256 devices in a mesh: leaf: 256 (over z, x, y, core).
Axes of the slice: x: 4, y: 4, z: 8, core: 2. Of those that a mesh axis runs over, the one named last changes fastest.
Arguments:
- coordinates: float32 [28, 524288], P(None, 'leaf'), may hold values from -6 to 6
- targets: float32 [32, 524288], P(None, 'leaf'), may hold values from -9 to 27
- anchor_index: int32 [8, 16384], P(None, 'leaf'), may hold values from 0 to 2047
Outputs:
- solution: float32 [32, 524288], P(None, 'leaf')
- residual: float32 [32, 524288], P(None, 'leaf')
The draws below stay inside these ranges and needn't reach their ends.
All inputs are finite; a program needn't handle non-finite values.
Results may differ from the reference program's by a relative error of at most 0.0003.
Values sent between devices are 32-bit elements; how exact they have to be, the bound alone decides.
No kernel may reach another device: no remote copies, remote signals or barrier semaphores. Data moves between devices by JAX's collectives and lax.ppermute only.
A program may use at most 64 MiB of HBM per device.

```python
import jax
import jax.numpy as jnp
from jax import lax

P_DEV = 2048
FEAT = 28
R = 64
NRHS = 32
ITERS = 2
LEVELS = 8
POINTS = 524288
N_LEAF = 256


def draw_coordinates(key, part):
    key = jax.random.fold_in(key, 5)
    values = jnp.clip(jax.random.normal(key, (FEAT, POINTS), jnp.float32), -6.0, 6.0)
    return values


def draw_targets(key, part):
    key = jax.random.fold_in(key, 11)
    ramp = 1.0 + 2.0 * jnp.arange(POINTS, dtype=jnp.float32) / POINTS
    base = jax.random.uniform(key, (NRHS, POINTS), jnp.float32, -1.0, 3.0)
    values = base * ramp[None, :]
    return values


def touch_ends(values, own_key, least, largest):
    shape = values.shape
    index_at = [jax.random.randint(jax.random.fold_in(own_key, axis), (), 0, shape[axis]) for axis in range(len(shape))]
    values = values.at[tuple(index_at)].set(least)
    longest = shape.index(max(shape))
    index_at[longest] = (index_at[longest] + 1) % shape[longest]
    return values.at[tuple(index_at)].set(largest)


def setup_inputs(seed: int = 0) -> dict:
    seeds = jax.random.split(jax.random.key(seed), 4)
    coordinates = draw_coordinates(jax.random.fold_in(seeds[3], 71), 0)
    targets = draw_targets(jax.random.fold_in(seeds[3], 71), 0)
    anchor_index = touch_ends(jax.random.randint(seeds[2], (LEVELS, R * N_LEAF), 0, P_DEV), jax.random.fold_in(seeds[2], 1), 0, P_DEV - 1).astype(jnp.int32)
    return dict(coordinates=coordinates, targets=targets, anchor_index=anchor_index)


HIGHEST = lax.Precision.HIGHEST


def kernel(left, right):
    inner_terms = jnp.dot(left.T, right, precision=HIGHEST, preferred_element_type=jnp.float32)
    dist_sq = jnp.sum(left * left, 0)[:, None] + jnp.sum(right * right, 0)[None, :] - 2.0 * inner_terms
    return jnp.exp(-2.0 * dist_sq / left.shape[0])


def swap_halves(stacked):
    shape = stacked.shape
    return stacked.reshape((shape[0] // 2, 2) + shape[1:])[:, ::-1].reshape(shape)


def pair_kernel(operands):
    return kernel(operands[0], operands[1])


def reference(coordinates, targets, anchor_index):
    total = P_DEV * N_LEAF
    columns = jnp.arange(R, dtype=jnp.int32)
    factors = []
    for level in range(LEVELS):
        group_span = 2 ** level
        groups = N_LEAF // group_span
        owner_dev = jnp.arange(groups, dtype=jnp.int32)[:, None] * group_span + (columns % group_span)[None, :]
        local_index = anchor_index[level].reshape(N_LEAF, R)[owner_dev, columns[None, :]]
        anchor_pts = coordinates[:, owner_dev * P_DEV + local_index].transpose(1, 0, 2)
        group_coords = coordinates.reshape(FEAT, groups, group_span * P_DEV).transpose(1, 0, 2)
        near_factor = lax.map(pair_kernel, (group_coords, anchor_pts))
        own_gram = lax.map(pair_kernel, (anchor_pts, anchor_pts))
        anchor_gram = lax.map(pair_kernel, (swap_halves(anchor_pts), anchor_pts))
        factors.append((near_factor, own_gram, anchor_gram))
    leaf_coords = coordinates.reshape(FEAT, N_LEAF, P_DEV).transpose(1, 0, 2)

    def leaf_term(operands):
        return jnp.dot(operands[1], kernel(operands[0], operands[0]), precision=HIGHEST, preferred_element_type=jnp.float32)

    def operator_apply(vector):
        leaf_vec = vector.reshape(NRHS, N_LEAF, P_DEV).transpose(1, 0, 2)
        leaf_part = lax.map(leaf_term, (leaf_coords, leaf_vec))
        result = vector + leaf_part.transpose(1, 0, 2).reshape(NRHS, total) * 0.25
        for level in range(LEVELS):
            near_factor, own_gram, anchor_gram = factors[level]
            group_span = 2 ** level
            groups = N_LEAF // group_span
            group_vec = vector.reshape(NRHS, groups, group_span * P_DEV).transpose(1, 0, 2)
            projected = jnp.einsum('gkn,gnr->gkr', group_vec, near_factor, precision=HIGHEST)
            mixed = jnp.einsum('gkr,grs->gks', projected, own_gram, precision=HIGHEST)
            mixed = mixed + jnp.einsum('gkr,grs->gks', swap_halves(projected), anchor_gram, precision=HIGHEST)
            coupled = jnp.einsum('gks,gns->gkn', mixed, near_factor, precision=HIGHEST)
            result = result + coupled.transpose(1, 0, 2).reshape(NRHS, total) * (512.0 / (R * group_span * P_DEV))
        return result

    solution = jnp.zeros_like(targets)
    residual = targets
    direction = targets
    norm_now = jnp.sum(residual * residual, 1)
    for iteration in range(ITERS):
        image = operator_apply(direction)
        alpha = norm_now / jnp.sum(direction * image, 1)
        solution = solution + alpha[:, None] * direction
        residual = residual - alpha[:, None] * image
        norm_next = jnp.sum(residual * residual, 1)
        direction = residual + (norm_next / norm_now)[:, None] * direction
        norm_now = norm_next
    return solution, residual
```

```python
import jax
import jax.numpy as jnp
from jax import lax
from jax.sharding import PartitionSpec as P

HIGHEST = lax.Precision.HIGHEST
HIGH = lax.Precision.HIGH
RANK = 64
ORDER = (6, 7, 5, 0, 3, 4, 1, 2)
PLACE = {level: divmod(spot, 2) for spot, level in enumerate(ORDER)}


def swapped(block, mask):
    count = lax.axis_size("leaf")
    return lax.ppermute(block, "leaf", [(i, i ^ mask) for i in range(count)])


def part(tiles, level):
    tile, side = PLACE[level]
    return tiles[tile, :, side * RANK : (side + 1) * RANK]


def kernel(left, right):
    inner = jnp.dot(left.T, right, precision=HIGHEST, preferred_element_type=jnp.float32)
    dist_sq = jnp.sum(left * left, 0)[:, None] + jnp.sum(right * right, 0)[None, :] - 2.0 * inner
    return jnp.exp(dist_sq * (-2.0 / 28.0))


def pair(me, level, near, far):
    upper = (me >> level) & 1
    return jnp.where(
        upper == 1, jnp.concatenate([far, near], 1), jnp.concatenate([near, far], 1)
    )


def exchange(me, tiles, scalars, visit):
    def add(tiles, extra):
        if extra is None:
            return tiles
        return tiles.at[1, :, RANK:].add(extra)

    if scalars is not None:
        both = jnp.concatenate([tiles, scalars[None]], 0)
        got = swapped(both, 1)
        scalars = scalars + got[4]
        got = got[:4]
    else:
        got = swapped(tiles, 1)
    extra = visit(0, [pair(me, 0, part(tiles, 0), part(got, 0))])
    tiles = tiles + got
    if scalars is not None:
        tiles = tiles.at[1, :, RANK:].set(scalars[:, :RANK] + extra)
    for count, level, masks in ((4, 1, (2, 4, 6)), (3, 3, (8, 16, 24)), (2, 5, (32,)), (2, 6, (64, 160, 192))):
        tiles = tiles[:count]
        got = [swapped(tiles, mask) for mask in masks]
        pairs = [pair(me, level, part(tiles, level), part(got[0], level))]
        if len(masks) == 3:
            pairs.append(pair(me, level, part(got[1], level), part(got[2], level)))
        extra = visit(level, pairs)
        tiles = tiles + got[0]
        if len(masks) == 3:
            other = got[1] + got[2]
            more = visit(level + 1, [pair(me, level + 1, part(tiles, level + 1), part(other, level + 1))])
            extra = None if extra is None else extra + more
            tiles = tiles + other
        tiles = add(tiles, extra)
    return tiles[1, :, RANK:]


def shards(coordinates, targets, anchor_index):
    feats, points = coordinates.shape
    me = lax.axis_index("leaf")
    order = jnp.array(ORDER, jnp.int32)
    columns = jnp.arange(RANK, dtype=jnp.int32)
    span = (1 << order)[:, None]
    mine = (columns[None, :] % span == me % span).reshape(-1)
    padded = jnp.concatenate([coordinates, jnp.zeros((32 - feats, points), jnp.float32)], 0)
    picked = padded[:, anchor_index[order, :].reshape(-1)]
    anchors = jnp.where(mine[None, :], picked, 0.0).reshape(32, 4, 128).transpose(1, 0, 2)

    anchor_pairs = {}

    def keep(level, pairs):
        anchor_pairs[level] = pairs

    exchange(me, anchors, None, keep)

    def own(level, both):
        upper = (me >> level) & 1
        return jnp.where(upper == 1, both[:, RANK:], both[:, :RANK])

    own_anchors = jnp.concatenate([own(level, anchor_pairs[level][0]) for level in ORDER], 1)
    near = kernel(padded, own_anchors)
    grams = {level: [kernel(z, z) for z in pairs] for level, pairs in anchor_pairs.items()}
    leaf = kernel(padded, padded)
    scale = {level: 512.0 / (RANK * (1 << level) * points) for level in ORDER}

    def project(vector):
        return jnp.dot(vector, near, precision=HIGHEST).reshape(32, 4, 128).transpose(1, 0, 2)

    def reduce(vector, scalars):
        mixed = {}

        def visit(level, pairs):
            total = 0.0
            for index, (both, gram) in enumerate(zip(pairs, grams[level])):
                image = jnp.dot(both, gram, precision=HIGHEST) * scale[level]
                total = total + jnp.sum(image * both, 1)
                if index == 0:
                    mixed[level] = own(level, image)
            return jnp.where(columns[None, :] == 0, total[:, None], 0.0)

        lanes = jnp.concatenate([jnp.stack(scalars, 1), jnp.zeros((32, 128 - len(scalars)), jnp.float32)], 1)
        sums = exchange(me, project(vector), lanes, visit)
        return sums, jnp.concatenate([mixed[level] for level in ORDER], 1)

    b = targets
    leaf_b = jnp.dot(b, leaf, precision=HIGH)
    v = b + 0.25 * leaf_b
    leaf_v = jnp.dot(v, leaf, precision=HIGH)
    leaf_near = jnp.dot(leaf, near, precision=HIGH)
    sums, mixed = reduce(b, [jnp.sum(b * v, 1), jnp.sum(b * b, 1)])
    bab, bb = sums[:, 0], sums[:, 1]
    alpha = (bb / bab)[:, None]
    w = v + jnp.dot(mixed, near.T, precision=HIGHEST)
    leaf_w = leaf_v + jnp.dot(mixed, leaf_near.T, precision=HIGHEST)
    r = b - alpha * w
    leaf_r = leaf_b - alpha * leaf_w
    ar = r + 0.25 * leaf_r
    sums, mixed = reduce(r, [jnp.sum(r * ar, 1), jnp.sum(r * r, 1), jnp.sum(r * w, 1)])
    rar, rr, rw = sums[:, 0], sums[:, 1], sums[:, 2]
    beta = rr / bb
    alpha_next = (rr / (rar + beta * (2.0 * rw + beta * bab)))[:, None]
    beta = beta[:, None]
    image = ar + jnp.dot(mixed, near.T, precision=HIGHEST) + beta * w
    return alpha * b + alpha_next * (r + beta * b), r - alpha_next * image


def solution(mesh):
    placed = P(None, "leaf")
    return jax.shard_map(
        shards,
        mesh=mesh,
        in_specs=(placed, placed, placed),
        out_specs=(placed, placed),
        check_vma=False,
    )
```

```python
import functools
import math

import jax
import jax.numpy as jnp
from jax import lax
from jax.experimental import pallas as pl
from jax.experimental.pallas import tpu as pltpu
from jax.sharding import PartitionSpec as P

F32 = jnp.float32
BF16 = jnp.bfloat16
RANK = 64
TILE = 128
TILES = 4
CHUNKS = 4
SIDE = 256
FEATS = 32
ORDER = (6, 7, 5, 0, 3, 4, 1, 2)
PLACE = {level: divmod(spot, 2) for spot, level in enumerate(ORDER)}
STAGES = ((4, 0, (1,)), (4, 1, (2, 4, 6)), (3, 3, (8, 16, 24)), (2, 5, (32,)), (2, 6, (64, 160, 192)))

VMEM = pl.BlockSpec(memory_space=pltpu.VMEM)
SMEM = pl.BlockSpec(memory_space=pltpu.SMEM)
HBM = pl.BlockSpec(memory_space=pltpu.HBM)


def call(body, outs, *args, spaces=None, out_spaces=None, scratch=(), mib=24):
    count = len(args)
    spaces = dict(spaces or {})
    out_spaces = dict(out_spaces or {})
    return pl.pallas_call(
        body,
        in_specs=[spaces.get(i, VMEM) for i in range(count)],
        out_specs=tuple(out_spaces.get(i, VMEM) for i in range(len(outs))),
        out_shape=tuple(outs),
        scratch_shapes=scratch,
        compiler_params=pltpu.CompilerParams(vmem_limit_bytes=mib << 20),
    )(*args)


def shape(*dims, dtype=F32):
    return jax.ShapeDtypeStruct(dims, dtype)


def split(x):
    high = x.astype(BF16)
    return high, (x - high.astype(F32)).astype(BF16)


def split3(x):
    high = x.astype(BF16)
    rest = x - high.astype(F32)
    middle = rest.astype(BF16)
    return high, middle, (rest - middle.astype(F32)).astype(BF16)


def dot(a, b):
    return jnp.dot(a, b, preferred_element_type=F32)


def dot_t(a, b):
    return lax.dot_general(a, b, (((1,), (1,)), ((), ())), preferred_element_type=F32)


def stack2(x):
    high, low = split(x)
    return high, jnp.concatenate([high, low], 0)


def three(high, two, u_high, u_low, product=dot):
    rows = high.shape[0]
    first = product(two, u_high)
    return first[:rows] + first[rows:] + product(high, u_low)


def padded(x):
    return jnp.concatenate([x, jnp.zeros((FEATS - x.shape[0], x.shape[1]), F32)], 0)


def both_sides(x, feats):
    x = x * math.sqrt(4.0 * math.log2(math.e) / feats)
    norm = -0.5 * jnp.sum(x * x, 0, keepdims=True)
    one, two, low = split3(x)
    row = lax.broadcasted_iota(jnp.int32, (SIDE - 6 * FEATS, x.shape[1]), 0)
    n1, n2, n3 = (jnp.broadcast_to(n.astype(F32), row.shape) for n in split3(norm))
    norms = jnp.where(row == 0, n1, jnp.where(row == 1, n2, jnp.where(row == 2, n3, 0.0)))
    end_left = jnp.where(row < 3, norms, jnp.where(row < 6, 1.0, 0.0)).astype(BF16)
    norms = jnp.where(row == 3, n1, jnp.where(row == 4, n2, jnp.where(row == 5, n3, 0.0)))
    end_right = jnp.where(row < 3, 1.0, norms).astype(BF16)
    left = jnp.concatenate([one, two, one, two, low, one, end_left], 0)
    right = jnp.concatenate([one, one, two, two, one, low, end_right], 0)
    return left, right


def turned(left):
    return left.astype(F32).T.astype(BF16)


def part(ref, level):
    tile, side = PLACE[level]
    return ref[tile, :, side * RANK : (side + 1) * RANK]


def upper(me_ref, level):
    return (me_ref[0] >> level) & 1 == 1


def pair(me_ref, level, near, far):
    high = upper(me_ref, level)
    return jnp.concatenate([jnp.where(high, far, near), jnp.where(high, near, far)], 1)


def start_body(me_ref, x_ref, index_ref, out_ref):
    parts = jnp.concatenate(split3(padded(x_ref[...])), 0)
    points = x_ref.shape[1]
    column = lax.broadcasted_iota(jnp.int32, (1, RANK), 1)
    row = lax.broadcasted_iota(jnp.int32, (points, TILE), 0)
    for tile in range(TILES):
        wanted = []
        for level in ORDER[2 * tile : 2 * tile + 2]:
            keep = (1 << level) - 1
            mine = (column & keep) == (me_ref[0] & keep)
            wanted.append(jnp.where(mine, index_ref[level : level + 1, :], -1))
        chosen = jnp.where(row == jnp.concatenate(wanted, 1), 1.0, 0.0).astype(BF16)
        got = dot(parts, chosen)
        out_ref[tile] = got[:FEATS] + got[FEATS : 2 * FEATS] + got[2 * FEATS :]


def prep_body(x_ref, left_ref, right_ref):
    left, right = both_sides(padded(x_ref[...]), x_ref.shape[0])
    left_ref[...] = turned(left)
    right_ref[...] = right


def leaf_body(chunk, left_ref, right_ref, b_ref, out_ref):
    rows, points = b_ref.shape
    width = points // CHUNKS
    columns = right_ref[:, chunk * width : (chunk + 1) * width]
    high, two = stack2(b_ref[...])
    total = jnp.zeros((rows, width), F32)
    for at in range(0, points, SIDE):
        here = slice(at, at + SIDE)
        k_high, k_low = split(jnp.exp2(dot(left_ref[here, :], columns)))
        total = total + three(high[:, here], two[:, here], k_high, k_low)
    out_ref[...] = total


def gram_body(feats, plan, me_ref, *refs):
    *refs, high_ref, low_ref = refs
    for index, (level, scale, near, far) in enumerate(plan):
        both = pair(me_ref, level, part(refs[near], level), part(refs[far], level))
        left, right = both_sides(both, feats)
        gram = jnp.exp2(dot(turned(left), right)) * scale
        high_ref[index], low_ref[index] = split(gram)


def near_body(feats, where, *refs):
    z_refs = refs[:8]
    right_ref, b_ref = refs[8:10]
    leaf_refs = refs[10 : 10 + CHUNKS]
    high_hbm, low_hbm, out_ref, v_ref, high_ref, low_ref, sems = refs[10 + CHUNKS :]
    rows, points = b_ref.shape
    width = points // CHUNKS
    z = jnp.concatenate([part(ref, level) for ref, level in zip(z_refs, ORDER)], 1)
    left = turned(both_sides(z, feats)[0])
    totals = jnp.zeros((rows, TILES * TILE), F32)
    bv = bb = jnp.zeros((rows, 1), F32)
    copies = []
    for chunk in range(CHUNKS):
        here = slice(chunk * width, (chunk + 1) * width)
        u_high, u_low = split(jnp.exp2(dot(left, right_ref[:, here])))
        high_ref[chunk] = u_high
        low_ref[chunk] = u_low
        for side, (source, target) in enumerate(((high_ref, high_hbm), (low_ref, low_hbm))):
            copy = pltpu.make_async_copy(source.at[chunk], target.at[chunk], sems.at[2 * chunk + side])
            copy.start()
            copies.append(copy)
        b = b_ref[:, here]
        b_high, two = stack2(b)
        totals = totals + three(b_high, two, u_high, u_low, dot_t)
        v = b + 0.25 * leaf_refs[chunk][...]
        v_ref[:, here] = v
        bv = bv + jnp.sum(b * v, 1, keepdims=True)
        bb = bb + jnp.sum(b * b, 1, keepdims=True)
    lane = lax.broadcasted_iota(jnp.int32, (rows, TILE), 1)
    for tile in range(TILES):
        out_ref[tile] = totals[:, tile * TILE : (tile + 1) * TILE]
    out_ref[TILES] = jnp.where(lane == 0, bv, jnp.where(lane == 1, bb, 0.0))
    for copy in copies:
        copy.wait()


def leaf_near_body(chunk, left_ref, right_ref, v_ref, high_hbm, low_hbm, *refs):
    out_high_hbm, out_low_hbm, out_v_ref, high_ref, low_ref, out_high_ref, out_low_ref, sems = refs
    rows, points = v_ref.shape
    width = points // CHUNKS
    rank = TILES * TILE
    copies = []
    for at in range(CHUNKS):
        here = slice(at * width, (at + 1) * width)
        for side, (source, target) in enumerate(((high_hbm, high_ref), (low_hbm, low_ref))):
            copy = pltpu.make_async_copy(source.at[at], target.at[:rank, here], sems.at[2 * at + side])
            copy.start()
            copies.append(copy)
    v_high, v_low = split(v_ref[...])
    high_ref[rank:, :] = v_high
    low_ref[rank:, :] = v_low
    for at in range(0, width, SIDE):
        start = chunk * width + at
        k_high, k_low = split(jnp.exp2(dot(left_ref[...], right_ref[:, start : start + SIDE])))
        if at == 0:
            for copy in copies:
                copy.wait()
        out = dot(high_ref[...], k_high) + dot(low_ref[...], k_high) + dot(high_ref[...], k_low)
        here = slice(at, at + SIDE)
        out_high_ref[:, here], out_low_ref[:, here] = split(out[:rank])
        out_v_ref[:, here] = out[rank:]
    copies = []
    for side, (source, target) in enumerate(((out_high_ref, out_high_hbm), (out_low_ref, out_low_hbm))):
        copy = pltpu.make_async_copy(source, target, sems.at[2 * CHUNKS + side])
        copy.start()
        copies.append(copy)
    for copy in copies:
        copy.wait()


def mix(me_ref, level, near, far, high_ref, low_ref, index):
    both = pair(me_ref, level, near, far)
    high, two = stack2(both)
    image = three(high, two, high_ref[index], low_ref[index])
    total = jnp.sum(image * both, 1, keepdims=True)
    mine = jnp.where(upper(me_ref, level), image[:, RANK:], image[:, :RANK])
    return mine, total


def sum_stage(stage, first, me_ref, tiles, gots, high_ref, low_ref):
    count, level, masks = STAGES[stage]
    index = first
    mine, total = mix(me_ref, level, part(tiles, level), part(gots[0], level), high_ref, low_ref, index)
    mixed = [mine]
    new = [tiles[i] + gots[0][i] for i in range(count)]
    if len(masks) == 3:
        index += 1
        _, more = mix(me_ref, level, part(gots[1], level), part(gots[2], level), high_ref, low_ref, index)
        total = total + more
        other = [gots[1][i] + gots[2][i] for i in range(count)]
        index += 1
        tile, side = PLACE[level + 1]
        here = slice(side * RANK, (side + 1) * RANK)
        mine, more = mix(me_ref, level + 1, new[tile][:, here], other[tile][:, here], high_ref, low_ref, index)
        mixed.append(mine)
        total = total + more
        new = [a + b for a, b in zip(new, other)]
    return new, mixed, total


def with_scalar(tile, total):
    lane = lax.broadcasted_iota(jnp.int32, tile.shape, 1)
    return tile + jnp.where(lane == RANK, total, 0.0)


def stage_body(stage, first, me_ref, *refs):
    masks = STAGES[stage][2]
    tiles, gots = refs[0], refs[1 : 1 + len(masks)]
    high_ref, low_ref, out_ref, mixed_ref = refs[1 + len(masks) :]
    new, mixed, total = sum_stage(stage, first, me_ref, tiles, gots, high_ref, low_ref)
    if stage == 0:
        scalars = tiles[TILES] + gots[0][TILES]
        new[1] = jnp.concatenate([new[1][:, :RANK], scalars[:, :RANK]], 1)
    new[1] = with_scalar(new[1], total)
    for tile in range(STAGES[stage + 1][0]):
        out_ref[tile] = new[tile]
    mixed_ref[...] = mixed[0] if len(mixed) == 1 else jnp.concatenate(mixed, 1)


def last_stage(first, refs):
    me_ref, tiles, *gots = refs[:5]
    high_ref, low_ref, m0_ref, m12_ref, m34_ref, m5_ref = refs[5:11]
    new, mixed, total = sum_stage(4, first, me_ref, tiles, gots, high_ref, low_ref)
    scalars = with_scalar(new[1], total)[:, RANK:]
    mixed = [*mixed, m5_ref[...], m0_ref[...], m34_ref[...], m12_ref[...]]
    return scalars, jnp.concatenate(mixed, 1)


def middle_body(first, *refs):
    scalars, mixed = last_stage(first, refs)
    refs = refs[11:]
    b_ref, v_ref, high_hbm, low_hbm = refs[:4]
    leaf_refs, near_refs = refs[4 : 4 + CHUNKS], refs[4 + CHUNKS : 4 + 4 * CHUNKS]
    out_ref, r_ref, w_ref, ar_ref, keep_ref, *buffers, sems = refs[4 + 4 * CHUNKS :]
    copies = []
    for chunk in range(CHUNKS):
        sources = (
            high_hbm.at[chunk], low_hbm.at[chunk], near_refs[3 * chunk], near_refs[3 * chunk + 1]
        )
        for side, source in enumerate(sources):
            copy = pltpu.make_async_copy(source, buffers[side].at[chunk], sems.at[4 * chunk + side])
            copy.start()
            copies.append(copy)
    bab, bb = scalars[:, 0:1], scalars[:, 1:2]
    alpha = bb / bab
    m_high, m_two = stack2(mixed)
    rows, points = b_ref.shape
    width = points // CHUNKS
    rar = rr = rw = jnp.zeros((rows, 1), F32)
    totals = jnp.zeros((rows, TILES * TILE), F32)
    for chunk in range(CHUNKS):
        here = slice(chunk * width, (chunk + 1) * width)
        for copy in copies[4 * chunk : 4 * chunk + 4]:
            copy.wait()
        high, low, n_high, n_low = (buffer[chunk] for buffer in buffers)
        w = v_ref[:, here] + three(m_high, m_two, high, low)
        leaf_w = near_refs[3 * chunk + 2][...] + three(m_high, m_two, n_high, n_low)
        r = b_ref[:, here] - alpha * w
        ar = r + 0.25 * (leaf_refs[chunk][...] - alpha * leaf_w)
        r_ref[:, here] = r
        w_ref[:, here] = w
        ar_ref[:, here] = ar
        rar = rar + jnp.sum(r * ar, 1, keepdims=True)
        rr = rr + jnp.sum(r * r, 1, keepdims=True)
        rw = rw + jnp.sum(r * w, 1, keepdims=True)
        r_high, r_two = stack2(r)
        totals = totals + three(r_high, r_two, high, low, dot_t)
    lane = lax.broadcasted_iota(jnp.int32, (rows, TILE), 1)
    for tile in range(TILES):
        out_ref[tile] = totals[:, tile * TILE : (tile + 1) * TILE]
    out_ref[TILES] = jnp.where(
        lane == 0, rar, jnp.where(lane == 1, rr, jnp.where(lane == 2, rw, 0.0))
    )
    keep_ref[...] = jnp.where(lane == 0, alpha, jnp.where(lane == 1, bab, jnp.where(lane == 2, bb, 0.0)))


def last_body(first, *refs):
    high_hbm, low_hbm, b_ref, r_ref, w_ref, ar_ref, keep_ref, x_ref, out_ref, *buffers, sems = refs[11:]
    copies = []
    for chunk in range(CHUNKS):
        for side, source in enumerate((high_hbm, low_hbm)):
            copy = pltpu.make_async_copy(source.at[chunk], buffers[side].at[chunk], sems.at[2 * chunk + side])
            copy.start()
            copies.append(copy)
    scalars, mixed = last_stage(first, refs)
    rar, rr, rw = scalars[:, 0:1], scalars[:, 1:2], scalars[:, 2:3]
    alpha, bab, bb = keep_ref[:, 0:1], keep_ref[:, 1:2], keep_ref[:, 2:3]
    beta = rr / bb
    alpha_next = rr / (rar + beta * (2.0 * rw + beta * bab))
    m_high, m_two = stack2(mixed)
    width = b_ref.shape[1] // CHUNKS
    for chunk in range(CHUNKS):
        here = slice(chunk * width, (chunk + 1) * width)
        for copy in copies[2 * chunk : 2 * chunk + 2]:
            copy.wait()
        r, b = r_ref[:, here], b_ref[:, here]
        image = ar_ref[:, here] + three(m_high, m_two, buffers[0][chunk], buffers[1][chunk])
        image = image + beta * w_ref[:, here]
        x_ref[:, here] = alpha * b + alpha_next * (r + beta * b)
        out_ref[:, here] = r - alpha_next * image


def swapped(block, mask):
    count = lax.axis_size("leaf")
    return lax.ppermute(block, "leaf", [(i, i ^ mask) for i in range(count)])


def send(stage, tiles, work):
    got = [swapped(tiles, mask) for mask in STAGES[stage][2]]
    if work is not None:
        *got, _ = lax.optimization_barrier((*got, work(tiles)))
    return got


def after(tiles, array):
    return lax.optimization_barrier((array, tiles))[0]


def shards(coordinates, targets, anchor_index):
    feats, points = coordinates.shape
    rows = targets.shape[0]
    width = points // CHUNKS
    rank = TILES * TILE
    b = targets
    me = lax.axis_index("leaf").astype(jnp.int32).reshape(1)
    scale = {level: 512.0 / (RANK * (1 << level) * points) for level in ORDER}

    (anchors,) = call(
        start_body, [shape(TILES, FEATS, TILE)], me, coordinates, anchor_index, spaces={0: SMEM}
    )

    left = right = None
    leaf_b = [None] * CHUNKS
    grams = [None, None]

    def leaf_chunk(chunk, tiles):
        (leaf_b[chunk],) = call(
            functools.partial(leaf_body, chunk), [shape(rows, width)], left, right, after(tiles, b)
        )
        return leaf_b[chunk]

    def prepare(tiles):
        nonlocal left, right
        left, right = call(
            prep_body,
            [shape(points, SIDE, dtype=BF16), shape(SIDE, points, dtype=BF16)],
            after(tiles, coordinates),
        )
        return leaf_chunk(0, tiles)

    def make_grams(which, stages, tiles):
        arrays, plan = [], []

        def add(level, near, far):
            plan.append((level, scale[level], len(arrays), len(arrays) + 1))
            arrays.extend((near, far))

        for stage in stages:
            level, masks = STAGES[stage][1:]
            own, gots, next_own, other = pieces[stage]
            add(level, own, gots[0])
            if len(masks) == 3:
                add(level, gots[1], gots[2])
                add(level + 1, next_own, other)
        out = shape(len(plan), TILE, TILE, dtype=BF16)
        grams[which] = call(
            functools.partial(gram_body, feats, tuple(plan)), [out, out], after(tiles, me), *arrays,
            spaces={0: SMEM},
        )
        return grams[which]

    def late_leaf(tiles):
        return make_grams(0, (0, 1, 2), tiles), leaf_chunk(2, tiles)

    work = {1: prepare, 2: functools.partial(leaf_chunk, 1), 3: late_leaf, 4: functools.partial(leaf_chunk, 3)}
    pieces = []
    tiles = anchors
    for stage, (count, level, masks) in enumerate(STAGES):
        tiles = tiles[:count]
        gots = send(stage, tiles, work.get(stage))
        new = tiles + gots[0]
        other = gots[1] + gots[2] if len(masks) == 3 else None
        pieces.append((tiles, gots, new, other))
        tiles = new if other is None else new + other
    holders = {0: pieces[0][0], 1: pieces[1][0], 2: pieces[1][2], 3: pieces[2][0], 4: pieces[2][2]}
    holders |= {5: pieces[3][0], 6: pieces[4][0], 7: pieces[4][2]}

    big = [shape(CHUNKS, rank, width, dtype=BF16)] * 2
    big_scratch = [pltpu.VMEM((CHUNKS, rank, width), BF16)] * 2
    high, low, message, v = call(
        functools.partial(near_body, feats, None),
        [*big, shape(TILES + 1, rows, TILE), shape(rows, points)],
        *[holders[level] for level in ORDER], right, b, *leaf_b,
        out_spaces={0: HBM, 1: HBM},
        scratch=[*big_scratch, pltpu.SemaphoreType.DMA((2 * CHUNKS,))],
    )

    def reduce(message, work):
        tiles = message
        mixed = []
        first = 0
        for stage, (count, level, masks) in enumerate(STAGES):
            gots = send(stage, tiles, work.get(stage))
            which, first = (0, (0, 1, 4)[stage]) if stage < 3 else (1, (0, 1)[stage - 3])
            if stage == 4:
                return first, [me, tiles, *gots, *grams[1], *mixed]
            tiles, coefs = call(
                functools.partial(stage_body, stage, first),
                [
                    shape(STAGES[stage + 1][0], rows, TILE),
                    shape(rows, RANK if len(masks) == 1 else TILE),
                ],
                me, tiles, *gots, *grams[which],
                spaces={0: SMEM},
            )
            mixed.append(coefs)

    leaf_near = [None] * CHUNKS

    def near_chunk(chunk, tiles):
        leaf_near[chunk] = call(
            functools.partial(leaf_near_body, chunk),
            [shape(rank, width, dtype=BF16), shape(rank, width, dtype=BF16), shape(rows, width)],
            left, right, after(tiles, v), high, low,
            spaces={3: HBM, 4: HBM},
            out_spaces={0: HBM, 1: HBM},
            scratch=[
                *[pltpu.VMEM((rank + rows, points), BF16)] * 2,
                *[pltpu.VMEM((rank, width), BF16)] * 2,
                pltpu.SemaphoreType.DMA((2 * CHUNKS + 2,)),
            ],
        )
        return leaf_near[chunk]

    def first_near(tiles):
        return make_grams(1, (3, 4), tiles), near_chunk(0, tiles)

    work = {stage: functools.partial(near_chunk, stage - 1) for stage in (2, 3, 4)}
    first, ends = reduce(message, {1: first_near, **work})
    args = [*ends, b, v, high, low, *leaf_b, *(piece for chunk in leaf_near for piece in chunk)]
    at = len(ends)
    spaces = {0: SMEM, at + 2: HBM, at + 3: HBM}
    for chunk in range(CHUNKS):
        for side in range(2):
            spaces[at + 4 + CHUNKS + 3 * chunk + side] = HBM
    message, r, w, ar, keep = call(
        functools.partial(middle_body, first),
        [shape(TILES + 1, rows, TILE), *[shape(rows, points)] * 3, shape(rows, TILE)],
        *args,
        spaces=spaces,
        scratch=[*big_scratch, *big_scratch, pltpu.SemaphoreType.DMA((4 * CHUNKS,))],
    )

    first, ends = reduce(message, {})
    return call(
        functools.partial(last_body, first),
        [shape(rows, points)] * 2,
        *ends, high, low, b, r, w, ar, keep,
        spaces={0: SMEM, at: HBM, at + 1: HBM},
        scratch=[*big_scratch, pltpu.SemaphoreType.DMA((2 * CHUNKS,))],
    )


def solution(mesh):
    placed = P(None, "leaf")
    return jax.shard_map(
        shards,
        mesh=mesh,
        in_specs=(placed, placed, placed),
        out_specs=(placed, placed),
        check_vma=False,
    )
```

```python
import functools
import math

import jax
import jax.numpy as jnp
from jax import lax
from jax.experimental import pallas as pl
from jax.experimental.pallas import tpu as pltpu
from jax.sharding import PartitionSpec as P

F32 = jnp.float32
BF16 = jnp.bfloat16
RANK = 64
TILE = 128
TILES = 4
CHUNKS = 4
SIDE = 256
FEATS = 32
ORDER = (6, 7, 5, 0, 3, 4, 1, 2)
PLACE = {level: divmod(spot, 2) for spot, level in enumerate(ORDER)}
STAGES = ((4, 0, (1,)), (4, 1, (2, 4, 6)), (3, 3, (8, 16, 24)), (2, 5, (32,)), (2, 6, (64, 160, 192)))

VMEM = pl.BlockSpec(memory_space=pltpu.VMEM)
SMEM = pl.BlockSpec(memory_space=pltpu.SMEM)


def call(body, outs, *args, spaces=None, aliases=None, mib=24):
    count = len(args)
    spaces = dict(spaces or {})
    return pl.pallas_call(
        body,
        in_specs=[spaces.get(i, VMEM) for i in range(count)],
        out_specs=(VMEM,) * len(outs),
        out_shape=tuple(outs),
        input_output_aliases=aliases or {},
        compiler_params=pltpu.CompilerParams(vmem_limit_bytes=mib << 20),
    )(*args)


def shape(*dims, dtype=F32):
    return jax.ShapeDtypeStruct(dims, dtype)


def split(x):
    high = x.astype(BF16)
    return high, (x - high.astype(F32)).astype(BF16)


def split3(x):
    high = x.astype(BF16)
    rest = x - high.astype(F32)
    middle = rest.astype(BF16)
    return high, middle, (rest - middle.astype(F32)).astype(BF16)


def dot(a, b):
    return jnp.dot(a, b, preferred_element_type=F32)


def dot_t(a, b):
    return lax.dot_general(a, b, (((1,), (1,)), ((), ())), preferred_element_type=F32)


def stack2(x):
    high, low = split(x)
    return high, jnp.concatenate([high, low], 0)


def three(high, two, u_high, u_low, product=dot):
    rows = high.shape[0]
    first = product(two, u_high)
    return first[:rows] + first[rows:] + product(high, u_low)


def padded(x):
    return jnp.concatenate([x, jnp.zeros((FEATS - x.shape[0], x.shape[1]), F32)], 0)


def both_sides(x, feats):
    x = x * math.sqrt(4.0 * math.log2(math.e) / feats)
    norm = -0.5 * jnp.sum(x * x, 0, keepdims=True)
    one, two, low = split3(x)
    row = lax.broadcasted_iota(jnp.int32, (SIDE - 6 * FEATS, x.shape[1]), 0)
    n1, n2, n3 = (jnp.broadcast_to(n.astype(F32), row.shape) for n in split3(norm))
    norms = jnp.where(row == 0, n1, jnp.where(row == 1, n2, jnp.where(row == 2, n3, 0.0)))
    end_left = jnp.where(row < 3, norms, jnp.where(row < 6, 1.0, 0.0)).astype(BF16)
    norms = jnp.where(row == 3, n1, jnp.where(row == 4, n2, jnp.where(row == 5, n3, 0.0)))
    end_right = jnp.where(row < 3, 1.0, norms).astype(BF16)
    left = jnp.concatenate([one, two, one, two, low, one, end_left], 0)
    right = jnp.concatenate([one, one, two, two, one, low, end_right], 0)
    return left, right


def turned(left):
    return left.astype(F32).T.astype(BF16)


def part(ref, level):
    tile, side = PLACE[level]
    return ref[tile, :, side * RANK : (side + 1) * RANK]


def upper(me_ref, level):
    return (me_ref[0] >> level) & 1 == 1


def pair(me_ref, level, near, far):
    high = upper(me_ref, level)
    return jnp.concatenate([jnp.where(high, far, near), jnp.where(high, near, far)], 1)


def start_body(me_ref, x_ref, index_ref, out_ref):
    parts = jnp.concatenate(split3(padded(x_ref[...])), 0)
    points = x_ref.shape[1]
    column = lax.broadcasted_iota(jnp.int32, (1, RANK), 1)
    row = lax.broadcasted_iota(jnp.int32, (points, TILE), 0)
    for tile in range(TILES):
        wanted = []
        for level in ORDER[2 * tile : 2 * tile + 2]:
            keep = (1 << level) - 1
            mine = (column & keep) == (me_ref[0] & keep)
            wanted.append(jnp.where(mine, index_ref[level : level + 1, :], -1))
        chosen = jnp.where(row == jnp.concatenate(wanted, 1), 1.0, 0.0).astype(BF16)
        got = dot(parts, chosen)
        out_ref[tile] = got[:FEATS] + got[FEATS : 2 * FEATS] + got[2 * FEATS :]


def prep_body(x_ref, left_ref, right_ref):
    left, right = both_sides(padded(x_ref[...]), x_ref.shape[0])
    left_ref[...] = turned(left)
    right_ref[...] = right


def leaf_body(blocks, left_ref, right_ref, b_ref, out_ref):
    rows, points = b_ref.shape
    width = points // CHUNKS
    high, two = stack2(b_ref[...])
    totals = [jnp.zeros((rows, width), F32)] * CHUNKS
    spans = [slice(i * width, (i + 1) * width) for i in range(CHUNKS)]
    for i, j in blocks:
        k_high, k_low = split(jnp.exp2(dot(left_ref[spans[i], :], right_ref[:, spans[j]])))
        totals[j] = totals[j] + three(high[:, spans[i]], two[:, spans[i]], k_high, k_low)
        if i != j:
            totals[i] = totals[i] + three(high[:, spans[j]], two[:, spans[j]], k_high, k_low, dot_t)
    for span, total in zip(spans, totals):
        out_ref[:, span] = total


def gram_body(feats, plan, me_ref, *refs):
    *refs, high_ref, low_ref = refs
    for index, (level, scale, near, far) in enumerate(plan):
        both = pair(me_ref, level, part(refs[near], level), part(refs[far], level))
        left, right = both_sides(both, feats)
        gram = jnp.exp2(dot(turned(left), right)) * scale
        high_ref[index], low_ref[index] = split(gram)


def near_tile(left, first, right_ref, b_ref, high_ref, low_ref):
    rows, points = b_ref.shape
    width = points // CHUNKS
    count = left.shape[0]
    total = jnp.zeros((rows, count), F32)
    for chunk in range(CHUNKS):
        here = slice(chunk * width, (chunk + 1) * width)
        u_high, u_low = split(jnp.exp2(dot(left, right_ref[:, here])))
        high_ref[first : first + count, here] = u_high
        low_ref[first : first + count, here] = u_low
        b_high, two = stack2(b_ref[:, here])
        total = total + three(b_high, two, u_high, u_low, dot_t)
    return total


def near_body(feats, *refs):
    z_refs, (right_ref, b_ref, high_ref, low_ref, out_ref) = refs[:6], refs[6:]
    z = jnp.concatenate([part(ref, level) for ref, level in zip(z_refs, ORDER[2:])], 1)
    left = turned(both_sides(z, feats)[0])
    total = near_tile(left, TILE, right_ref, b_ref, high_ref, low_ref)
    for tile in range(TILES - 1):
        out_ref[tile] = total[:, tile * TILE : (tile + 1) * TILE]


def far_body(feats, z6_ref, z7_ref, right_ref, b_ref, lower_ref, *refs):
    leaf_refs = refs[:CHUNKS]
    high_ref, low_ref, out_ref, v_ref, leaf_ref, z_ref = refs[CHUNKS + 2 :]
    rows, points = b_ref.shape
    rank = TILES * TILE
    z = jnp.concatenate([part(z6_ref, 6), part(z7_ref, 7)], 1)
    z_ref[0] = z
    left = turned(both_sides(z, feats)[0])
    out_ref[0] = near_tile(left, 0, right_ref, b_ref, high_ref, low_ref)
    for tile in range(TILES - 1):
        out_ref[1 + tile] = lower_ref[tile]
    b = b_ref[...]
    leaf = (leaf_refs[0][...] + leaf_refs[1][...]) + (leaf_refs[2][...] + leaf_refs[3][...])
    leaf_ref[...] = leaf
    v = b + 0.25 * leaf
    v_ref[...] = v
    high_ref[rank:, :], low_ref[rank:, :] = split(v)
    bv = jnp.sum(b * v, 1, keepdims=True)
    bb = jnp.sum(b * b, 1, keepdims=True)
    lane = lax.broadcasted_iota(jnp.int32, (rows, TILE), 1)
    out_ref[TILES] = jnp.where(lane == 0, bv, jnp.where(lane == 1, bb, 0.0))


def leaf_near_body(chunk, left_ref, right_ref, high_ref, low_ref, out_high_ref, out_low_ref, out_v_ref):
    width = right_ref.shape[1] // CHUNKS
    rank = TILES * TILE
    for at in range(0, width, SIDE):
        start = chunk * width + at
        k_high, k_low = split(jnp.exp2(dot(left_ref[...], right_ref[:, start : start + SIDE])))
        out = dot(high_ref[...], k_high) + dot(low_ref[...], k_high) + dot(high_ref[...], k_low)
        here = slice(at, at + SIDE)
        out_high_ref[:, here], out_low_ref[:, here] = split(out[:rank])
        out_v_ref[:, here] = out[rank:]


def mix(me_ref, level, near, far, gram):
    both = pair(me_ref, level, near, far)
    high, two = stack2(both)
    image = three(high, two, *gram)
    total = jnp.sum(image * both, 1, keepdims=True)
    mine = jnp.where(upper(me_ref, level), image[:, RANK:], image[:, :RANK])
    return mine, total


def sum_stage(stage, me_ref, tiles, gots, grams):
    count, level, masks = STAGES[stage]
    mine, total = mix(me_ref, level, part(tiles, level), part(gots[0], level), grams[0])
    mixed = [mine]
    new = [tiles[i] + gots[0][i] for i in range(count)]
    if len(masks) == 3:
        _, more = mix(me_ref, level, part(gots[1], level), part(gots[2], level), grams[1])
        total = total + more
        other = [gots[1][i] + gots[2][i] for i in range(count)]
        tile, side = PLACE[level + 1]
        here = slice(side * RANK, (side + 1) * RANK)
        mine, more = mix(me_ref, level + 1, new[tile][:, here], other[tile][:, here], grams[2])
        mixed.append(mine)
        total = total + more
        new = [a + b for a, b in zip(new, other)]
    return new, mixed, total


def with_scalar(tile, total):
    lane = lax.broadcasted_iota(jnp.int32, tile.shape, 1)
    return tile + jnp.where(lane == RANK, total, 0.0)


def stage_body(stage, first, me_ref, *refs):
    masks = STAGES[stage][2]
    tiles, gots = refs[0], refs[1 : 1 + len(masks)]
    high_ref, low_ref, *more, out_ref, mixed_ref = refs[1 + len(masks) :]
    grams = [(high_ref[first + i], low_ref[first + i]) for i in range(len(masks))]
    new, mixed, total = sum_stage(stage, me_ref, tiles, gots, grams)
    if stage == 0:
        scalars = tiles[TILES] + gots[0][TILES]
        new[1] = jnp.concatenate([new[1][:, :RANK], scalars[:, :RANK]], 1)
    new[1] = with_scalar(new[1], total)
    for tile in range(STAGES[stage + 1][0]):
        out_ref[tile] = new[tile]
    for ref in more:
        out_ref[STAGES[stage + 1][0]] = ref[0]
    mixed_ref[...] = mixed[0] if len(mixed) == 1 else jnp.concatenate(mixed, 1)


def last_stage(refs, late):
    me_ref, tiles, *gots = refs[:5]
    high_ref, low_ref, m0_ref, m12_ref, m34_ref, m5_ref = refs[5:11]
    new, mixed, total = sum_stage(4, me_ref, tiles, gots, [(high_ref[1], low_ref[1]), *late])
    scalars = with_scalar(new[1], total)[:, RANK:]
    mixed = [*mixed, m5_ref[...], m0_ref[...], m34_ref[...], m12_ref[...]]
    return scalars, jnp.concatenate(mixed, 1)


def middle_body(feats, scales, *refs):
    me_ref, tiles, _, got_near, got_far = refs[:5]
    z_ref, b_ref, v_ref, leaf_ref, high_ref, low_ref = refs[11:17]
    near_refs = refs[17 : 17 + 3 * CHUNKS]
    out_ref, r_ref, w_ref, ar_ref, keep_ref, late_high_ref, late_low_ref = refs[17 + 3 * CHUNKS :]
    late = []
    for index, (level, near, far) in enumerate(
        ((6, got_near[2], got_far[2]), (7, z_ref[0], got_near[2]))
    ):
        side = PLACE[level][1]
        here = slice(side * RANK, (side + 1) * RANK)
        left, right = both_sides(pair(me_ref, level, near[:, here], far[:, here]), feats)
        late.append(split(jnp.exp2(dot(turned(left), right)) * scales[index]))
        late_high_ref[index], late_low_ref[index] = late[index]
    scalars, mixed = last_stage(refs, late)
    bab, bb = scalars[:, 0:1], scalars[:, 1:2]
    alpha = bb / bab
    m_high, m_two = stack2(mixed)
    rows, points = b_ref.shape
    width = points // CHUNKS
    rank = TILES * TILE
    rar = rr = rw = jnp.zeros((rows, 1), F32)
    totals = jnp.zeros((rows, rank), F32)
    for chunk in range(CHUNKS):
        here = slice(chunk * width, (chunk + 1) * width)
        high, low = high_ref[:rank, here], low_ref[:rank, here]
        w = v_ref[:, here] + three(m_high, m_two, high, low)
        r = b_ref[:, here] - alpha * w
        r_ref[:, here] = r
        w_ref[:, here] = w
        r_high, r_two = stack2(r)
        totals = totals + three(r_high, r_two, high, low, dot_t)
        n_high, n_low, n_v = (ref[...] for ref in near_refs[3 * chunk : 3 * chunk + 3])
        leaf_w = n_v + three(m_high, m_two, n_high, n_low)
        ar = r + 0.25 * (leaf_ref[:, here] - alpha * leaf_w)
        ar_ref[:, here] = ar
        rar = rar + jnp.sum(r * ar, 1, keepdims=True)
        rr = rr + jnp.sum(r * r, 1, keepdims=True)
        rw = rw + jnp.sum(r * w, 1, keepdims=True)
    lane = lax.broadcasted_iota(jnp.int32, (rows, TILE), 1)
    for tile in range(TILES):
        out_ref[tile] = totals[:, tile * TILE : (tile + 1) * TILE]
    out_ref[TILES] = jnp.where(
        lane == 0, rar, jnp.where(lane == 1, rr, jnp.where(lane == 2, rw, 0.0))
    )
    keep_ref[...] = jnp.where(lane == 0, alpha, jnp.where(lane == 1, bab, jnp.where(lane == 2, bb, 0.0)))


def last_body(*refs):
    late_high_ref, late_low_ref, high_ref, low_ref, b_ref, r_ref, w_ref, ar_ref, keep_ref, x_ref, out_ref = refs[11:]
    late = [(late_high_ref[i], late_low_ref[i]) for i in range(2)]
    scalars, mixed = last_stage(refs, late)
    rar, rr, rw = scalars[:, 0:1], scalars[:, 1:2], scalars[:, 2:3]
    alpha, bab, bb = keep_ref[:, 0:1], keep_ref[:, 1:2], keep_ref[:, 2:3]
    beta = rr / bb
    alpha_next = rr / (rar + beta * (2.0 * rw + beta * bab))
    m_high, m_two = stack2(mixed)
    width = b_ref.shape[1] // CHUNKS
    rank = TILES * TILE
    for chunk in range(CHUNKS):
        here = slice(chunk * width, (chunk + 1) * width)
        r, b = r_ref[:, here], b_ref[:, here]
        image = ar_ref[:, here] + three(m_high, m_two, high_ref[:rank, here], low_ref[:rank, here])
        image = image + beta * w_ref[:, here]
        x_ref[:, here] = alpha * b + alpha_next * (r + beta * b)
        out_ref[:, here] = r - alpha_next * image


def swapped(block, mask):
    count = lax.axis_size("leaf")
    return lax.ppermute(block, "leaf", [(i, i ^ mask) for i in range(count)])


def send(stage, tiles, work, masks):
    got = [swapped(tiles, mask) for mask in masks]
    if work is not None:
        *got, _ = lax.optimization_barrier((*got, work(tiles)))
    return got


def after(tiles, array):
    return lax.optimization_barrier((array, tiles))[0]


def shards(coordinates, targets, anchor_index):
    feats, points = coordinates.shape
    rows = targets.shape[0]
    width = points // CHUNKS
    rank = TILES * TILE
    b = targets
    me = lax.axis_index("leaf").astype(jnp.int32).reshape(1)
    scale = {level: 512.0 / (RANK * (1 << level) * points) for level in ORDER}

    (anchors,) = call(
        start_body, [shape(TILES, FEATS, TILE)], me, coordinates, anchor_index,
        spaces={0: SMEM},
    )

    left = right = lower = None
    leaf_b = []
    grams = [None, None]

    def leaf_blocks(blocks, tiles):
        leaf_b.extend(
            call(
                functools.partial(leaf_body, blocks), [shape(rows, points)], left, right, after(tiles, b)
            )
        )
        return leaf_b[-1]

    def prepare(tiles):
        nonlocal left, right
        left, right = call(
            prep_body,
            [shape(points, SIDE, dtype=BF16), shape(SIDE, points, dtype=BF16)],
            after(tiles, coordinates),
        )
        return leaf_blocks(((0, 0), (0, 1), (1, 1)), tiles)

    def make_grams(which, stages, tiles):
        arrays, plan = [], []

        def add(level, near, far):
            plan.append((level, scale[level], len(arrays), len(arrays) + 1))
            arrays.extend((near, far))

        for stage in stages:
            level = STAGES[stage][1]
            own, gots, next_own, other = pieces[stage]
            add(level, own, gots[0])
            if len(gots) == 3:
                add(level, gots[1], gots[2])
                add(level + 1, next_own, other)
        out = shape(len(plan), TILE, TILE, dtype=BF16)
        grams[which] = call(
            functools.partial(gram_body, feats, tuple(plan)), [out, out], after(tiles, me), *arrays,
            spaces={0: SMEM},
        )
        return grams[which]

    def third(tiles):
        return make_grams(0, (0, 1, 2), tiles), leaf_blocks(((0, 2), (2, 2)), tiles)

    def fourth(tiles):
        nonlocal lower
        holders = {0: pieces[0][0], 1: pieces[1][0], 2: pieces[1][2], 3: pieces[2][0], 4: pieces[2][2]}
        holders |= {5: pieces[3][0]}
        big = shape(rank + rows, points, dtype=BF16)
        lower = call(
            functools.partial(near_body, feats),
            [big, big, shape(TILES - 1, rows, TILE)],
            *[holders[level] for level in ORDER[2:]], right, after(tiles, b),
        )
        return leaf_blocks(((2, 3), (3, 3)), tiles), lower

    work = {
        1: prepare,
        2: functools.partial(leaf_blocks, ((0, 3), (1, 2), (1, 3))),
        3: third,
        4: fourth,
    }
    pieces = []
    tiles = anchors
    for stage, (count, level, masks) in enumerate(STAGES):
        last = stage == 4
        tiles = tiles[: 1 if last else count]
        gots = send(stage, tiles, work.get(stage), masks[:1] if last else masks)
        new = tiles + gots[0]
        other = gots[1] + gots[2] if len(gots) == 3 else None
        pieces.append((tiles, gots, new, other))
        tiles = new if other is None else new + other

    high, low, lower_tiles = lower
    big = shape(rank + rows, points, dtype=BF16)
    at = 5 + len(leaf_b)
    high, low, message, v, leaf_sum, z_tile = call(
        functools.partial(far_body, feats),
        [big, big, shape(TILES + 1, rows, TILE), *[shape(rows, points)] * 2, shape(1, FEATS, TILE)],
        pieces[4][0], pieces[4][2], right, b, lower_tiles, *leaf_b, high, low,
        aliases={at: 0, at + 1: 1},
    )

    def reduce(message, work, extra):
        tiles = message
        mixed = []
        for stage, (count, level, masks) in enumerate(STAGES):
            gots = send(stage, tiles, work.get(stage), masks)
            if stage == 4:
                return [me, tiles, *gots, *grams[1], *mixed]
            more = extra if stage == 3 else []
            tiles, coefs = call(
                functools.partial(stage_body, stage, (0, 1, 4, 0)[stage]),
                [
                    shape(STAGES[stage + 1][0] + len(more), rows, TILE),
                    shape(rows, RANK if len(masks) == 1 else TILE),
                ],
                me, tiles, *gots, *grams[stage // 3], *more,
                spaces={0: SMEM},
            )
            mixed.append(coefs)

    leaf_near = [None] * CHUNKS

    def near_chunk(chunk, tiles):
        leaf_near[chunk] = call(
            functools.partial(leaf_near_body, chunk),
            [shape(rank, width, dtype=BF16), shape(rank, width, dtype=BF16), shape(rows, width)],
            left, after(tiles, right), high, low,
        )
        return leaf_near[chunk]

    def first_near(tiles):
        return make_grams(1, (3, 4), tiles), near_chunk(0, tiles)

    work = {stage: functools.partial(near_chunk, stage - 1) for stage in (2, 3, 4)}
    ends = reduce(message, {1: first_near, **work}, [z_tile])
    args = [*ends, z_tile, b, v, leaf_sum, high, low, *(piece for chunk in leaf_near for piece in chunk)]
    late = shape(2, TILE, TILE, dtype=BF16)
    message, r, w, ar, keep, *late = call(
        functools.partial(middle_body, feats, (scale[6], scale[7])),
        [shape(TILES + 1, rows, TILE), *[shape(rows, points)] * 3, shape(rows, TILE), late, late],
        *args,
        spaces={0: SMEM},
    )

    ends = reduce(message, {}, [])
    return call(
        last_body, [shape(rows, points)] * 2, *ends, *late, high, low, b, r, w, ar, keep, spaces={0: SMEM}
    )


def solution(mesh):
    placed = P(None, "leaf")
    return jax.shard_map(
        shards,
        mesh=mesh,
        in_specs=(placed, placed, placed),
        out_specs=(placed, placed),
        check_vma=False,
    )
```

```python
import functools
import math

import jax
import jax.numpy as jnp
from jax import lax
from jax.experimental import pallas as pl
from jax.experimental.pallas import tpu as pltpu
from jax.sharding import PartitionSpec as P

F32 = jnp.float32
BF16 = jnp.bfloat16
RANK = 64
TILE = 128
TILES = 4
CHUNKS = 4
SIDE = 256
FEATS = 32
ORDER = (6, 7, 5, 0, 3, 4, 1, 2)
SENT = (7, 0, 5, 6, 3, 4, 1, 2)
PLACE = {level: divmod(spot, 2) for spot, level in enumerate(SENT)}
STAGES = ((4, 0, (1,)), (4, 1, (2, 4, 6)), (3, 3, (8, 16, 24)), (2, 5, (32, 64, 96)), (1, 7, (192,)))
LAST = len(STAGES) - 1
ENDS = 7

VMEM = pl.BlockSpec(memory_space=pltpu.VMEM)
SMEM = pl.BlockSpec(memory_space=pltpu.SMEM)
ANY = pl.BlockSpec(memory_space=pl.ANY)


def call(body, outs, *args, spaces=None, aliases=None, mib=10):
    count = len(args)
    spaces = dict(spaces or {})
    return pl.pallas_call(
        body,
        in_specs=[spaces.get(i, VMEM) for i in range(count)],
        out_specs=(VMEM,) * len(outs),
        out_shape=tuple(outs),
        input_output_aliases=aliases or {},
        compiler_params=pltpu.CompilerParams(vmem_limit_bytes=mib << 20),
    )(*args)


def shape(*dims, dtype=F32):
    return jax.ShapeDtypeStruct(dims, dtype)


def split(x):
    high = x.astype(BF16)
    return high, (x - high.astype(F32)).astype(BF16)


def split3(x):
    high = x.astype(BF16)
    rest = x - high.astype(F32)
    middle = rest.astype(BF16)
    return high, middle, (rest - middle.astype(F32)).astype(BF16)


def dot(a, b):
    return jnp.dot(a, b, preferred_element_type=F32)


def dot_t(a, b):
    return lax.dot_general(a, b, (((1,), (1,)), ((), ())), preferred_element_type=F32)


def stack2(x):
    high, low = split(x)
    return high, jnp.concatenate([high, low], 0)


def three(high, two, u_high, u_low, product=dot):
    rows = high.shape[0]
    first = product(two, u_high)
    return first[:rows] + first[rows:] + product(high, u_low)


def padded(x):
    return jnp.concatenate([x, jnp.zeros((FEATS - x.shape[0], x.shape[1]), F32)], 0)


def both_sides(x, feats):
    x = x * math.sqrt(4.0 * math.log2(math.e) / feats)
    norm = -0.5 * jnp.sum(x * x, 0, keepdims=True)
    one, two, low = split3(x)
    row = lax.broadcasted_iota(jnp.int32, (SIDE - 6 * FEATS, x.shape[1]), 0)
    n1, n2, n3 = (jnp.broadcast_to(n.astype(F32), row.shape) for n in split3(norm))
    norms = jnp.where(row == 0, n1, jnp.where(row == 1, n2, jnp.where(row == 2, n3, 0.0)))
    end_left = jnp.where(row < 3, norms, jnp.where(row < 6, 1.0, 0.0)).astype(BF16)
    norms = jnp.where(row == 3, n1, jnp.where(row == 4, n2, jnp.where(row == 5, n3, 0.0)))
    end_right = jnp.where(row < 3, 1.0, norms).astype(BF16)
    left = jnp.concatenate([one, two, one, two, low, one, end_left], 0)
    right = jnp.concatenate([one, one, two, two, one, low, end_right], 0)
    return left, right


def turned(left):
    return left.astype(F32).T.astype(BF16)


def part(ref, level):
    tile, side = PLACE[level]
    return ref[tile, :, side * RANK : (side + 1) * RANK]


def upper(me_ref, level):
    return (me_ref[0] >> level) & 1 == 1


def pair(me_ref, level, near, far):
    high = upper(me_ref, level)
    return jnp.concatenate([jnp.where(high, far, near), jnp.where(high, near, far)], 1)


def start_body(me_ref, x_ref, index_ref, out_ref, copy_ref):
    x = padded(x_ref[...])
    copy_ref[...] = x
    parts = jnp.concatenate(split3(x), 0)
    points = x_ref.shape[1]
    column = lax.broadcasted_iota(jnp.int32, (1, RANK), 1)
    row = lax.broadcasted_iota(jnp.int32, (points, TILE), 0)
    for tile in range(TILES):
        wanted = []
        for level in SENT[2 * tile : 2 * tile + 2]:
            keep = (1 << level) - 1
            mine = (column & keep) == (me_ref[0] & keep)
            wanted.append(jnp.where(mine, index_ref[level : level + 1, :], -1))
        chosen = jnp.where(row == jnp.concatenate(wanted, 1), 1.0, 0.0).astype(BF16)
        got = dot(parts, chosen)
        out_ref[tile] = got[:FEATS] + got[FEATS : 2 * FEATS] + got[2 * FEATS :]


def prep_body(feats, x_ref, b_ref, _, left_ref, right_ref, copy_ref):
    copy_ref[...] = b_ref[...]
    left, right = both_sides(x_ref[...], feats)
    left_ref[...] = turned(left)
    right_ref[...] = right


def leaf_body(blocks, left_ref, right_ref, b_ref, _, *refs):
    out_ref, high_ref, low_ref = refs[-3:]
    rows, points = b_ref.shape
    width = points // CHUNKS
    high, two = stack2(b_ref[...])
    totals = [jnp.zeros((rows, width), F32)] * CHUNKS
    spans = [slice(i * width, (i + 1) * width) for i in range(CHUNKS)]
    for i, j in blocks:
        k_high, k_low = split(jnp.exp2(dot(left_ref[spans[i], :], right_ref[:, spans[j]])))
        high_ref[spans[i], spans[j]] = k_high
        low_ref[spans[i], spans[j]] = k_low
        totals[j] = totals[j] + three(high[:, spans[i]], two[:, spans[i]], k_high, k_low)
        if i != j:
            totals[i] = totals[i] + three(high[:, spans[j]], two[:, spans[j]], k_high, k_low, dot_t)
    for span, total in zip(spans, totals):
        out_ref[:, span] = total


def gram_body(feats, plan, me_ref, _, *refs):
    *refs, high_ref, low_ref = refs
    for index, (level, scale, near, far) in enumerate(plan):
        both = pair(me_ref, level, part(refs[near], level), part(refs[far], level))
        left, right = both_sides(both, feats)
        gram = jnp.exp2(dot(turned(left), right)) * scale
        high_ref[index], low_ref[index] = split(gram)


def near_tile(left, first, right_ref, b_ref, high_ref, low_ref):
    rows, points = b_ref.shape
    width = points // CHUNKS
    count = left.shape[0]
    total = jnp.zeros((rows, count), F32)
    for chunk in range(CHUNKS):
        here = slice(chunk * width, (chunk + 1) * width)
        u_high, u_low = split(jnp.exp2(dot(left, right_ref[:, here])))
        high_ref[first : first + count, here] = u_high
        low_ref[first : first + count, here] = u_low
        b_high, two = stack2(b_ref[:, here])
        total = total + three(b_high, two, u_high, u_low, dot_t)
    return total


def near_body(feats, *refs):
    z_refs, (right_ref, b_ref), (high_ref, low_ref, out_ref) = refs[:6], refs[6:8], refs[8:]
    z = jnp.concatenate([part(ref, level) for ref, level in zip(z_refs, ORDER[2:])], 1)
    left = turned(both_sides(z, feats)[0])
    out_ref[...] = near_tile(left, TILE, right_ref, b_ref, high_ref, low_ref)


def put_tiles(out_ref, total):
    for tile in range(TILES):
        halves = []
        for level in SENT[2 * tile : 2 * tile + 2]:
            at = ORDER.index(level) * RANK
            halves.append(total[:, at : at + RANK])
        out_ref[tile] = jnp.concatenate(halves, 1)


def far_body(feats, z6_ref, z7_ref, right_ref, b_ref, lower_ref, *refs):
    leaf_refs, (high_ref, low_ref, out_ref, v_ref, leaf_ref, z_ref) = refs[:-8], refs[-6:]
    rank = TILES * TILE
    rows = b_ref.shape[0]
    z = jnp.concatenate([part(z6_ref, 6), part(z7_ref, 7)], 1)
    z_ref[0] = z
    left = turned(both_sides(z, feats)[0])
    total = near_tile(left, 0, right_ref, b_ref, high_ref, low_ref)
    put_tiles(out_ref, jnp.concatenate([total, lower_ref[...]], 1))
    b = b_ref[...]
    leaf = leaf_refs[0][...]
    for ref in leaf_refs[1:]:
        leaf = leaf + ref[...]
    leaf_ref[...] = leaf
    v = b + 0.25 * leaf
    v_ref[...] = v
    high_ref[rank:, :], low_ref[rank:, :] = split(v)
    bv = jnp.sum(b * v, 1, keepdims=True)
    bb = jnp.sum(b * b, 1, keepdims=True)
    lane = lax.broadcasted_iota(jnp.int32, (rows, TILE), 1)
    out_ref[TILES] = jnp.where(lane == 0, bv, jnp.where(lane == 1, bb, 0.0))


def leaf_near_body(blocks, k_high_ref, k_low_ref, high_ref, low_ref, _, *refs):
    out_high_ref, out_low_ref, out_v_ref = refs[-3:]
    points = k_high_ref.shape[0]
    width = points // CHUNKS
    rank = TILES * TILE
    for block in blocks:
        span = slice(block * SIDE, (block + 1) * SIDE)
        end = (block * SIDE // width + 1) * width
        k_high, k_low = k_high_ref[:end, span], k_low_ref[:end, span]
        high, low = high_ref[:, :end], low_ref[:, :end]
        out = dot(high, k_high) + dot(low, k_high) + dot(high, k_low)
        if end < points:
            k_high, k_low = k_high_ref[span, end:], k_low_ref[span, end:]
            high, low = high_ref[:, end:], low_ref[:, end:]
            out = out + dot_t(high, k_high) + dot_t(low, k_high) + dot_t(high, k_low)
        out_high_ref[:, span], out_low_ref[:, span] = split(out[:rank])
        out_v_ref[:, span] = out[rank:]


def mix(me_ref, level, near, far, gram):
    both = pair(me_ref, level, near, far)
    high, two = stack2(both)
    image = three(high, two, *gram)
    total = jnp.sum(image * both, 1, keepdims=True)
    mine = jnp.where(upper(me_ref, level), image[:, RANK:], image[:, :RANK])
    return mine, total


def sum_stage(stage, me_ref, tiles, gots, grams):
    count, level, masks = STAGES[stage]
    mine, total = mix(me_ref, level, part(tiles, level), part(gots[0], level), grams[0])
    mixed = [mine]
    new = [tiles[i] + gots[0][i] for i in range(count)]
    if len(masks) == 3:
        _, more = mix(me_ref, level, part(gots[1], level), part(gots[2], level), grams[1])
        total = total + more
        other = [gots[1][i] + gots[2][i] for i in range(count)]
        tile, side = PLACE[level + 1]
        here = slice(side * RANK, (side + 1) * RANK)
        mine, more = mix(me_ref, level + 1, new[tile][:, here], other[tile][:, here], grams[2])
        mixed.append(mine)
        total = total + more
        new = [a + b for a, b in zip(new, other)]
    return new, mixed, total


def with_scalar(tile, total):
    lane = lax.broadcasted_iota(jnp.int32, tile.shape, 1)
    return tile + jnp.where(lane == RANK, total, 0.0)


def stage_body(stage, first, me_ref, *refs):
    masks = STAGES[stage][2]
    tiles, gots = refs[0], refs[1 : 1 + len(masks)][::-1]
    high_ref, low_ref, *more, out_ref, mixed_ref = refs[1 + len(masks) :]
    grams = [(high_ref[first + i], low_ref[first + i]) for i in range(len(masks))]
    new, mixed, total = sum_stage(stage, me_ref, tiles, gots, grams)
    if stage == 0:
        scalars = tiles[TILES] + gots[0][TILES]
        new[0] = jnp.concatenate([new[0][:, :RANK], scalars[:, :RANK]], 1)
    new[0] = with_scalar(new[0], total)
    for tile in range(STAGES[stage + 1][0]):
        out_ref[tile] = new[tile]
    for ref in more:
        out_ref[STAGES[stage + 1][0]] = ref[0]
    mixed_ref[...] = mixed[0] if len(mixed) == 1 else jnp.concatenate(mixed, 1)


def last_stage(refs, late):
    me_ref, tiles, got, m0_ref, m12_ref, m34_ref, m56_ref = refs
    new, (m7,), total = sum_stage(LAST, me_ref, tiles, [got], [late])
    scalars = with_scalar(new[0], total)[:, RANK:]
    m5, m6 = m56_ref[:, :RANK], m56_ref[:, RANK:]
    return scalars, jnp.concatenate([m6, m7, m5, m0_ref[...], m34_ref[...], m12_ref[...]], 1)


def middle_body(feats, scale, *refs):
    ends, refs = refs[:ENDS], refs[ENDS:]
    z_ref, b_ref, v_ref, leaf_ref, high_ref, low_ref, near_high_ref, near_low_ref, near_v_ref = refs[:9]
    out_ref, r_ref, w_ref, ar_ref, keep_ref, late_high_ref, late_low_ref = refs[9:]
    here = slice(RANK, 2 * RANK)
    both = pair(ends[0], STAGES[LAST][1], z_ref[0][:, here], ends[2][1][:, here])
    left, right = both_sides(both, feats)
    late = split(jnp.exp2(dot(turned(left), right)) * scale)
    late_high_ref[...], late_low_ref[...] = late
    scalars, mixed = last_stage(ends, late)
    bab, bb = scalars[:, 0:1], scalars[:, 1:2]
    alpha = bb / bab
    m_high, m_two = stack2(mixed)
    rows, points = b_ref.shape
    width = points // CHUNKS
    rank = TILES * TILE
    rar = rr = rw = jnp.zeros((rows, 1), F32)
    totals = jnp.zeros((rows, rank), F32)
    for chunk in range(CHUNKS):
        here = slice(chunk * width, (chunk + 1) * width)
        high, low = high_ref[:rank, here], low_ref[:rank, here]
        w = v_ref[:, here] + three(m_high, m_two, high, low)
        r = b_ref[:, here] - alpha * w
        r_ref[:, here] = r
        w_ref[:, here] = w
        r_high, r_two = stack2(r)
        totals = totals + three(r_high, r_two, high, low, dot_t)
        leaf_w = near_v_ref[:, here] + three(m_high, m_two, near_high_ref[:, here], near_low_ref[:, here])
        ar = r + 0.25 * (leaf_ref[:, here] - alpha * leaf_w)
        ar_ref[:, here] = ar
        rar = rar + jnp.sum(r * ar, 1, keepdims=True)
        rr = rr + jnp.sum(r * r, 1, keepdims=True)
        rw = rw + jnp.sum(r * w, 1, keepdims=True)
    lane = lax.broadcasted_iota(jnp.int32, (rows, TILE), 1)
    put_tiles(out_ref, totals)
    out_ref[TILES] = jnp.where(
        lane == 0, rar, jnp.where(lane == 1, rr, jnp.where(lane == 2, rw, 0.0))
    )
    keep_ref[...] = jnp.where(lane == 0, alpha, jnp.where(lane == 1, bab, jnp.where(lane == 2, bb, 0.0)))


def last_body(*refs):
    ends, late, refs = refs[:ENDS], refs[ENDS : ENDS + 2], refs[ENDS + 2 :]
    high_ref, low_ref, b_ref, r_ref, w_ref, ar_ref, keep_ref, x_ref, out_ref = refs
    scalars, mixed = last_stage(ends, [ref[...] for ref in late])
    rar, rr, rw = scalars[:, 0:1], scalars[:, 1:2], scalars[:, 2:3]
    alpha, bab, bb = keep_ref[:, 0:1], keep_ref[:, 1:2], keep_ref[:, 2:3]
    beta = rr / bb
    alpha_next = rr / (rar + beta * (2.0 * rw + beta * bab))
    m_high, m_two = stack2(mixed)
    width = b_ref.shape[1] // CHUNKS
    rank = TILES * TILE
    for chunk in range(CHUNKS):
        here = slice(chunk * width, (chunk + 1) * width)
        r, b = r_ref[:, here], b_ref[:, here]
        image = ar_ref[:, here] + three(m_high, m_two, high_ref[:rank, here], low_ref[:rank, here])
        image = image + beta * w_ref[:, here]
        x_ref[:, here] = alpha * b + alpha_next * (r + beta * b)
        out_ref[:, here] = r - alpha_next * image


def swapped(block, mask):
    count = lax.axis_size("leaf")
    return lax.ppermute(block, "leaf", [(i, i ^ mask) for i in range(count)])


def send(stage, tiles, work, masks):
    got = [swapped(tiles, mask) for mask in masks[::-1]]
    if work is not None:
        *got, _ = lax.optimization_barrier((*got, work(tiles)))
    return got[::-1]


def shards(coordinates, targets, anchor_index):
    feats, points = coordinates.shape
    rows = targets.shape[0]
    width = points // CHUNKS
    rank = TILES * TILE
    b = None
    me = lax.axis_index("leaf").astype(jnp.int32).reshape(1)
    scale = {level: 512.0 / (RANK * (1 << level) * points) for level in ORDER}

    anchors, x = call(
        start_body, [shape(TILES, FEATS, TILE), shape(FEATS, points)], me, coordinates, anchor_index,
        spaces={0: SMEM},
    )

    left = right = None
    leaf_b = []
    kept = []
    lower = None
    near = []
    grams = [None, None]

    def leaf_blocks(blocks, tiles):
        nonlocal kept
        square = shape(points, points, dtype=BF16)
        out, *kept = call(
            functools.partial(leaf_body, blocks),
            [shape(rows, points), square, square],
            left, right, b, tiles, *kept,
            spaces={3: ANY},
            aliases={4: 1, 5: 2} if kept else None,
        )
        leaf_b.append(out)
        return out

    def make_near(pieces):
        nonlocal near, lower
        holders = [pieces[3][0], pieces[0][0], pieces[2][0], pieces[2][2], pieces[1][0], pieces[1][2]]
        big = shape(rank + rows, points, dtype=BF16)
        *near, lower = call(
            functools.partial(near_body, feats), [big, big, shape(rows, rank - TILE)], *holders, right, b
        )
        return lower

    def prepare(tiles):
        nonlocal left, right, b
        left, right, b = call(
            functools.partial(prep_body, feats),
            [shape(points, SIDE, dtype=BF16), shape(SIDE, points, dtype=BF16), shape(rows, points)],
            x, targets, tiles,
            spaces={2: ANY},
        )
        return leaf_blocks(((0, 0), (0, 1), (1, 1)), tiles)

    def make_grams(which, stages, tiles):
        arrays, plan = [], []

        def add(level, near, far):
            plan.append((level, scale[level], len(arrays), len(arrays) + 1))
            arrays.extend((near, far))

        for stage in stages:
            level = STAGES[stage][1]
            own, gots, next_own, other = pieces[stage]
            add(level, own, gots[0])
            if len(gots) == 3:
                add(level, gots[1], gots[2])
                add(level + 1, next_own, other)
        out = shape(len(plan), TILE, TILE, dtype=BF16)
        grams[which] = call(
            functools.partial(gram_body, feats, tuple(plan)), [out, out], me, tiles, *arrays,
            spaces={0: SMEM, 1: ANY},
        )
        return grams[which]

    def last_near(tiles):
        pieces.append((tiles,))
        lower = make_near(pieces)
        pieces.pop()
        return lower, leaf_blocks(((2, 3), (3, 3)), tiles), make_grams(0, (0, 1, 2), tiles)

    work = {
        1: prepare,
        2: functools.partial(leaf_blocks, ((0, 2), (0, 3), (1, 2), (1, 3), (2, 2))),
        3: last_near,
    }
    pieces = []
    tiles = anchors
    for stage, (count, level, masks) in enumerate(STAGES[:LAST]):
        tiles = tiles[:count]
        gots = send(stage, tiles, work.get(stage), masks)
        new = tiles + gots[0]
        other = gots[2] + gots[1] if len(gots) == 3 else None
        pieces.append((tiles, gots, new, other))
        tiles = new if other is None else new + other

    big = shape(rank + rows, points, dtype=BF16)
    at = 5 + len(leaf_b)
    high, low, message, v, leaf_sum, z_tile = call(
        functools.partial(far_body, feats),
        [big, big, shape(TILES + 1, rows, TILE), *[shape(rows, points)] * 2, shape(1, FEATS, TILE)],
        pieces[3][2], tiles, right, b, lower, *leaf_b, *near,
        aliases={at: 0, at + 1: 1},
    )

    def reduce(message, work, extra):
        tiles = message
        mixed = []
        for stage, (count, level, masks) in enumerate(STAGES):
            gots = send(stage, tiles, work.get(stage), masks)
            if stage == LAST:
                return [me, tiles, *gots, *mixed]
            more = extra if stage == LAST - 1 else []
            which, first = ((0, 0), (0, 1), (0, 4), (1, 0))[stage]
            tiles, coefs = call(
                functools.partial(stage_body, stage, first),
                [
                    shape(STAGES[stage + 1][0] + len(more), rows, TILE),
                    shape(rows, RANK if len(masks) == 1 else TILE),
                ],
                me, tiles, *gots[::-1], *grams[which], *more,
                spaces={0: SMEM},
            )
            mixed.append(coefs)

    leaf_near = []

    def near_blocks(blocks, tiles):
        nonlocal leaf_near
        wide = shape(rank, points, dtype=BF16)
        leaf_near = call(
            functools.partial(leaf_near_body, blocks),
            [wide, wide, shape(rows, points)],
            *kept, high, low, tiles, *leaf_near,
            spaces={4: ANY},
            aliases={5: 0, 6: 1, 7: 2} if leaf_near else None,
        )
        return leaf_near

    def first_near(tiles):
        return make_grams(1, (3,), tiles), near_blocks((0, 1), tiles)

    work = {1: first_near}
    for stage, blocks in ((2, (2, 3)), (3, (4, 5)), (4, (6, 7))):
        work[stage] = functools.partial(near_blocks, blocks)
    ends = reduce(message, work, [z_tile])
    late = shape(TILE, TILE, dtype=BF16)
    message, r, w, ar, keep, *late = call(
        functools.partial(middle_body, feats, scale[7]),
        [shape(TILES + 1, rows, TILE), *[shape(rows, points)] * 3, shape(rows, TILE), late, late],
        *ends, z_tile, b, v, leaf_sum, high, low, *leaf_near,
        spaces={0: SMEM},
    )

    ends = reduce(message, {}, [])
    return call(
        last_body, [shape(rows, points)] * 2, *ends, *late, high, low, b, r, w, ar, keep, spaces={0: SMEM}
    )


def solution(mesh):
    placed = P(None, "leaf")
    return jax.shard_map(
        shards,
        mesh=mesh,
        in_specs=(placed, placed, placed),
        out_specs=(placed, placed),
        check_vma=False,
    )
```

```python
import functools
import math

import jax
import jax.numpy as jnp
from jax import lax
from jax.experimental import pallas as pl
from jax.experimental.pallas import tpu as pltpu
from jax.sharding import PartitionSpec as P

F32 = jnp.float32
BF16 = jnp.bfloat16
F8 = jnp.float8_e4m3fn
LIFT = 2.0**8
LIFT_LOW = 2.0**16
RANK = 64
TILE = 128
TILES = 4
CHUNKS = 4
SIDE = 256
FEATS = 32
ORDER = (6, 7, 5, 0, 3, 4, 1, 2)
SENT = (7, 0, 5, 6, 3, 4, 1, 2)
PLACE = {level: divmod(spot, 2) for spot, level in enumerate(SENT)}
STAGES = ((4, 0, (1,)), (4, 1, (2, 4, 6)), (3, 3, (8, 16, 24)), (2, 5, (32, 64, 96)), (1, 7, (192,)))
LAST = len(STAGES) - 1
ENDS = 7

VMEM = pl.BlockSpec(memory_space=pltpu.VMEM)
SMEM = pl.BlockSpec(memory_space=pltpu.SMEM)
ANY = pl.BlockSpec(memory_space=pl.ANY)


def call(body, outs, *args, spaces=None, aliases=None, mib=10):
    count = len(args)
    spaces = dict(spaces or {})
    return pl.pallas_call(
        body,
        in_specs=[spaces.get(i, VMEM) for i in range(count)],
        out_specs=(VMEM,) * len(outs),
        out_shape=tuple(outs),
        input_output_aliases=aliases or {},
        compiler_params=pltpu.CompilerParams(vmem_limit_bytes=mib << 20),
    )(*args)


def shape(*dims, dtype=F32):
    return jax.ShapeDtypeStruct(dims, dtype)


def split(x):
    high = x.astype(BF16)
    return high, (x - high.astype(F32)).astype(BF16)


def split3(x):
    high = x.astype(BF16)
    rest = x - high.astype(F32)
    middle = rest.astype(BF16)
    return high, middle, (rest - middle.astype(F32)).astype(BF16)


def eighths(high, low):
    return (high * LIFT).astype(F8), (low * LIFT_LOW).astype(F8)


def dot(a, b):
    return jnp.dot(a, b, preferred_element_type=F32)


def dot_t(a, b):
    return lax.dot_general(a, b, (((1,), (1,)), ((), ())), preferred_element_type=F32)


def stack2(x):
    high, low = split(x)
    return high, jnp.concatenate([high, low], 0)


def three(high, two, u_high, u_low, product=dot):
    rows = high.shape[0]
    first = product(two, u_high)
    return first[:rows] + first[rows:] + product(high, u_low)


def padded(x):
    return jnp.concatenate([x, jnp.zeros((FEATS - x.shape[0], x.shape[1]), F32)], 0)


def both_sides(x, feats):
    x = x * math.sqrt(4.0 * math.log2(math.e) / feats)
    norm = -0.5 * jnp.sum(x * x, 0, keepdims=True)
    one, two, low = split3(x)
    row = lax.broadcasted_iota(jnp.int32, (SIDE - 6 * FEATS, x.shape[1]), 0)
    n1, n2, n3 = (jnp.broadcast_to(n.astype(F32), row.shape) for n in split3(norm))
    norms = jnp.where(row == 0, n1, jnp.where(row == 1, n2, jnp.where(row == 2, n3, 0.0)))
    end_left = jnp.where(row < 3, norms, jnp.where(row < 6, 1.0, 0.0)).astype(BF16)
    norms = jnp.where(row == 3, n1, jnp.where(row == 4, n2, jnp.where(row == 5, n3, 0.0)))
    end_right = jnp.where(row < 3, 1.0, norms).astype(BF16)
    left = jnp.concatenate([one, two, one, two, low, one, end_left], 0)
    right = jnp.concatenate([one, one, two, two, one, low, end_right], 0)
    return left, right


def turned(left):
    return left.astype(F32).T.astype(BF16)


def part(ref, level):
    tile, side = PLACE[level]
    return ref[tile, :, side * RANK : (side + 1) * RANK]


def upper(me_ref, level):
    return (me_ref[0] >> level) & 1 == 1


def pair(me_ref, level, near, far):
    high = upper(me_ref, level)
    return jnp.concatenate([jnp.where(high, far, near), jnp.where(high, near, far)], 1)


def start_body(me_ref, x_ref, index_ref, out_ref, copy_ref):
    x = padded(x_ref[...])
    copy_ref[...] = x
    parts = jnp.concatenate(split3(x), 0)
    points = x_ref.shape[1]
    column = lax.broadcasted_iota(jnp.int32, (1, RANK), 1)
    row = lax.broadcasted_iota(jnp.int32, (points, TILE), 0)
    for tile in range(TILES):
        wanted = []
        for level in SENT[2 * tile : 2 * tile + 2]:
            keep = (1 << level) - 1
            mine = (column & keep) == (me_ref[0] & keep)
            wanted.append(jnp.where(mine, index_ref[level : level + 1, :], -1))
        chosen = jnp.where(row == jnp.concatenate(wanted, 1), 1.0, 0.0).astype(BF16)
        got = dot(parts, chosen)
        out_ref[tile] = got[:FEATS] + got[FEATS : 2 * FEATS] + got[2 * FEATS :]


def prep_body(feats, x_ref, b_ref, _, left_ref, right_ref, copy_ref):
    copy_ref[...] = b_ref[...]
    left, right = both_sides(x_ref[...], feats)
    left_ref[...] = turned(left)
    right_ref[...] = right


def leaf_body(blocks, left_ref, right_ref, b_ref, _, *refs):
    out_ref, high_ref, high8_ref, low8_ref = refs[-4:]
    rows, points = b_ref.shape
    width = points // CHUNKS
    high, two = stack2(b_ref[...])
    totals = [jnp.zeros((rows, width), F32)] * CHUNKS
    spans = [slice(i * width, (i + 1) * width) for i in range(CHUNKS)]
    for i, j in blocks:
        k_high, k_low = split(jnp.exp2(dot(left_ref[spans[i], :], right_ref[:, spans[j]])))
        high_ref[spans[i], spans[j]] = k_high
        high8_ref[spans[i], spans[j]], low8_ref[spans[i], spans[j]] = eighths(k_high, k_low)
        totals[j] = totals[j] + three(high[:, spans[i]], two[:, spans[i]], k_high, k_low)
        if i != j:
            totals[i] = totals[i] + three(high[:, spans[j]], two[:, spans[j]], k_high, k_low, dot_t)
    for span, total in zip(spans, totals):
        out_ref[:, span] = total


def gram_body(feats, plan, me_ref, _, *refs):
    *refs, high_ref, low_ref = refs
    for index, (level, scale, near, far) in enumerate(plan):
        both = pair(me_ref, level, part(refs[near], level), part(refs[far], level))
        left, right = both_sides(both, feats)
        gram = jnp.exp2(dot(turned(left), right)) * scale
        high_ref[index], low_ref[index] = split(gram)


def near_tile(left, first, right_ref, b_ref, high_ref, low_ref, high8_ref, low8_ref):
    rows, points = b_ref.shape
    width = points // CHUNKS
    count = left.shape[0]
    total = jnp.zeros((rows, count), F32)
    for chunk in range(CHUNKS):
        here = slice(chunk * width, (chunk + 1) * width)
        u_high, u_low = split(jnp.exp2(dot(left, right_ref[:, here])))
        at = slice(first, first + count)
        high_ref[at, here], low_ref[at, here] = u_high, u_low
        high8_ref[at, here], low8_ref[at, here] = eighths(u_high, u_low)
        b_high, two = stack2(b_ref[:, here])
        total = total + three(b_high, two, u_high, u_low, dot_t)
    return total


def near_body(feats, *refs):
    z_refs, (right_ref, b_ref), (*near_refs, out_ref) = refs[:6], refs[6:8], refs[8:]
    z = jnp.concatenate([part(ref, level) for ref, level in zip(z_refs, ORDER[2:])], 1)
    left = turned(both_sides(z, feats)[0])
    out_ref[...] = near_tile(left, TILE, right_ref, b_ref, *near_refs)


def put_tiles(out_ref, total):
    for tile in range(TILES):
        halves = []
        for level in SENT[2 * tile : 2 * tile + 2]:
            at = ORDER.index(level) * RANK
            halves.append(total[:, at : at + RANK])
        out_ref[tile] = jnp.concatenate(halves, 1)


def far_body(feats, z6_ref, z7_ref, right_ref, b_ref, lower_ref, *refs):
    leaf_refs, near_refs, (out_ref, v_ref, leaf_ref, z_ref, most_ref) = refs[:-13], refs[-9:-5], refs[-5:]
    rank = TILES * TILE
    rows = b_ref.shape[0]
    z = jnp.concatenate([part(z6_ref, 6), part(z7_ref, 7)], 1)
    z_ref[0] = z
    left = turned(both_sides(z, feats)[0])
    total = near_tile(left, 0, right_ref, b_ref, *near_refs)
    put_tiles(out_ref, jnp.concatenate([total, lower_ref[...]], 1))
    b = b_ref[...]
    leaf = leaf_refs[0][...]
    for ref in leaf_refs[1:]:
        leaf = leaf + ref[...]
    leaf_ref[...] = leaf
    v = b + 0.25 * leaf
    v_ref[...] = v
    most = jnp.max(jnp.abs(v), 1, keepdims=True)
    most = jnp.where(most > 0.0, most, 1.0)
    most_ref[...] = jnp.broadcast_to(most, most_ref.shape)
    high_ref, _, high8_ref, _ = near_refs
    _, v_two = stack2(v)
    high_ref[rank:, :] = v_two
    high8_ref[rank:, :] = (v * (LIFT / most)).astype(F8)
    bv = jnp.sum(b * v, 1, keepdims=True)
    bb = jnp.sum(b * b, 1, keepdims=True)
    lane = lax.broadcasted_iota(jnp.int32, (rows, TILE), 1)
    out_ref[TILES] = jnp.where(lane == 0, bv, jnp.where(lane == 1, bb, 0.0))


def leaf_near_body(blocks, k_ref, k_high8_ref, k_low8_ref, high_ref, high8_ref, low8_ref, most_ref, _, *refs):
    out_high_ref, out_low_ref, out_v_ref = refs[-3:]
    points = k_ref.shape[0]
    width = points // CHUNKS
    rank = TILES * TILE
    rows = out_v_ref.shape[0]
    for block in blocks:
        span = slice(block * SIDE, (block + 1) * SIDE)
        end = (block * SIDE // width + 1) * width
        out = dot(high_ref[:, :end], k_ref[:end, span])
        second = dot(high8_ref[:, :end], k_low8_ref[:end, span])
        other = dot(low8_ref[:, :end], k_high8_ref[:end, span])
        if end < points:
            out = out + dot_t(high_ref[:, end:], k_ref[span, end:])
            second = second + dot_t(high8_ref[:, end:], k_low8_ref[span, end:])
            other = other + dot_t(low8_ref[:, end:], k_high8_ref[span, end:])
        scale = 1.0 / (LIFT * LIFT_LOW)
        out_high_ref[:, span], out_low_ref[:, span] = split(out[:rank] + (second[:rank] + other) * scale)
        last = out[rank : rank + rows] + out[rank + rows :]
        out_v_ref[:, span] = last + (most_ref[:, :1] * scale) * second[rank:]


def mix(me_ref, level, near, far, gram):
    both = pair(me_ref, level, near, far)
    high, two = stack2(both)
    image = three(high, two, *gram)
    total = jnp.sum(image * both, 1, keepdims=True)
    mine = jnp.where(upper(me_ref, level), image[:, RANK:], image[:, :RANK])
    return mine, total


def sum_stage(stage, me_ref, tiles, gots, grams):
    count, level, masks = STAGES[stage]
    mine, total = mix(me_ref, level, part(tiles, level), part(gots[0], level), grams[0])
    mixed = [mine]
    new = [tiles[i] + gots[0][i] for i in range(count)]
    if len(masks) == 3:
        _, more = mix(me_ref, level, part(gots[1], level), part(gots[2], level), grams[1])
        total = total + more
        other = [gots[1][i] + gots[2][i] for i in range(count)]
        tile, side = PLACE[level + 1]
        here = slice(side * RANK, (side + 1) * RANK)
        mine, more = mix(me_ref, level + 1, new[tile][:, here], other[tile][:, here], grams[2])
        mixed.append(mine)
        total = total + more
        new = [a + b for a, b in zip(new, other)]
    return new, mixed, total


def with_scalar(tile, total):
    lane = lax.broadcasted_iota(jnp.int32, tile.shape, 1)
    return tile + jnp.where(lane == RANK, total, 0.0)


def stage_body(stage, first, me_ref, *refs):
    masks = STAGES[stage][2]
    tiles, gots = refs[0], refs[1 : 1 + len(masks)][::-1]
    high_ref, low_ref, *more, out_ref, mixed_ref = refs[1 + len(masks) :]
    grams = [(high_ref[first + i], low_ref[first + i]) for i in range(len(masks))]
    new, mixed, total = sum_stage(stage, me_ref, tiles, gots, grams)
    if stage == 0:
        scalars = tiles[TILES] + gots[0][TILES]
        new[0] = jnp.concatenate([new[0][:, :RANK], scalars[:, :RANK]], 1)
    new[0] = with_scalar(new[0], total)
    for tile in range(STAGES[stage + 1][0]):
        out_ref[tile] = new[tile]
    for ref in more:
        out_ref[STAGES[stage + 1][0]] = ref[0]
    mixed_ref[...] = mixed[0] if len(mixed) == 1 else jnp.concatenate(mixed, 1)


def last_stage(refs, late):
    me_ref, tiles, got, m0_ref, m12_ref, m34_ref, m56_ref = refs
    new, (m7,), total = sum_stage(LAST, me_ref, tiles, [got], [late])
    scalars = with_scalar(new[0], total)[:, RANK:]
    m5, m6 = m56_ref[:, :RANK], m56_ref[:, RANK:]
    return scalars, jnp.concatenate([m6, m7, m5, m0_ref[...], m34_ref[...], m12_ref[...]], 1)


def middle_body(feats, scale, *refs):
    ends, refs = refs[:ENDS], refs[ENDS:]
    z_ref, b_ref, v_ref, leaf_ref, high_ref, low_ref, near_high_ref, near_low_ref, near_v_ref = refs[:9]
    out_ref, r_ref, w_ref, ar_ref, keep_ref, late_high_ref, late_low_ref = refs[9:]
    here = slice(RANK, 2 * RANK)
    both = pair(ends[0], STAGES[LAST][1], z_ref[0][:, here], ends[2][1][:, here])
    left, right = both_sides(both, feats)
    late = split(jnp.exp2(dot(turned(left), right)) * scale)
    late_high_ref[...], late_low_ref[...] = late
    scalars, mixed = last_stage(ends, late)
    bab, bb = scalars[:, 0:1], scalars[:, 1:2]
    alpha = bb / bab
    m_high, m_two = stack2(mixed)
    rows, points = b_ref.shape
    width = points // CHUNKS
    rank = TILES * TILE
    rar = rr = rw = jnp.zeros((rows, 1), F32)
    totals = jnp.zeros((rows, rank), F32)
    for chunk in range(CHUNKS):
        here = slice(chunk * width, (chunk + 1) * width)
        high, low = high_ref[:rank, here], low_ref[:rank, here]
        w = v_ref[:, here] + three(m_high, m_two, high, low)
        r = b_ref[:, here] - alpha * w
        r_ref[:, here] = r
        w_ref[:, here] = w
        r_high, r_two = stack2(r)
        totals = totals + three(r_high, r_two, high, low, dot_t)
        leaf_w = near_v_ref[:, here] + three(m_high, m_two, near_high_ref[:, here], near_low_ref[:, here])
        ar = r + 0.25 * (leaf_ref[:, here] - alpha * leaf_w)
        ar_ref[:, here] = ar
        rar = rar + jnp.sum(r * ar, 1, keepdims=True)
        rr = rr + jnp.sum(r * r, 1, keepdims=True)
        rw = rw + jnp.sum(r * w, 1, keepdims=True)
    lane = lax.broadcasted_iota(jnp.int32, (rows, TILE), 1)
    put_tiles(out_ref, totals)
    out_ref[TILES] = jnp.where(
        lane == 0, rar, jnp.where(lane == 1, rr, jnp.where(lane == 2, rw, 0.0))
    )
    keep_ref[...] = jnp.where(lane == 0, alpha, jnp.where(lane == 1, bab, jnp.where(lane == 2, bb, 0.0)))


def image_body(m0_ref, m12_ref, m34_ref, m56_ref, ar_ref, high_ref, low_ref, _, out_ref):
    m5, m6 = m56_ref[:, :RANK], m56_ref[:, RANK:]
    mixed = [m6, jnp.zeros_like(m6), m5, m0_ref[...], m34_ref[...], m12_ref[...]]
    m_high, m_two = stack2(jnp.concatenate(mixed, 1))
    rank = TILES * TILE
    width = ar_ref.shape[1] // CHUNKS
    for chunk in range(CHUNKS):
        here = slice(chunk * width, (chunk + 1) * width)
        out_ref[:, here] = ar_ref[:, here] + three(m_high, m_two, high_ref[:rank, here], low_ref[:rank, here])


def last_body(*refs):
    ends, late, refs = refs[:ENDS], refs[ENDS : ENDS + 2], refs[ENDS + 2 :]
    high_ref, low_ref, b_ref, r_ref, w_ref, image_ref, keep_ref, x_ref, out_ref = refs
    scalars, mixed = last_stage(ends, [ref[...] for ref in late])
    rar, rr, rw = scalars[:, 0:1], scalars[:, 1:2], scalars[:, 2:3]
    alpha, bab, bb = keep_ref[:, 0:1], keep_ref[:, 1:2], keep_ref[:, 2:3]
    beta = rr / bb
    alpha_next = rr / (rar + beta * (2.0 * rw + beta * bab))
    m7 = mixed[:, RANK : 2 * RANK]
    m_high, m_two = stack2(jnp.concatenate([jnp.zeros_like(m7), m7], 1))
    width = b_ref.shape[1] // CHUNKS
    for chunk in range(CHUNKS):
        here = slice(chunk * width, (chunk + 1) * width)
        r, b = r_ref[:, here], b_ref[:, here]
        image = image_ref[:, here] + three(m_high, m_two, high_ref[:TILE, here], low_ref[:TILE, here])
        image = image + beta * w_ref[:, here]
        x_ref[:, here] = alpha * b + alpha_next * (r + beta * b)
        out_ref[:, here] = r - alpha_next * image


def swapped(block, mask):
    count = lax.axis_size("leaf")
    return lax.ppermute(block, "leaf", [(i, i ^ mask) for i in range(count)])


def send(stage, tiles, work, masks):
    got = [swapped(tiles, mask) for mask in masks[::-1]]
    if work is not None:
        *got, _ = lax.optimization_barrier((*got, work(tiles)))
    return got[::-1]


def shards(coordinates, targets, anchor_index):
    feats, points = coordinates.shape
    rows = targets.shape[0]
    width = points // CHUNKS
    rank = TILES * TILE
    b = None
    me = lax.axis_index("leaf").astype(jnp.int32).reshape(1)
    scale = {level: 512.0 / (RANK * (1 << level) * points) for level in ORDER}

    anchors, x = call(
        start_body,
        [shape(TILES, FEATS, TILE), shape(FEATS, points)],
        me, coordinates, anchor_index,
        spaces={0: SMEM},
    )

    left = right = None
    leaf_b = []
    kept = []
    bigs = [
        shape(rank + 2 * rows, points, dtype=BF16),
        shape(rank, points, dtype=BF16),
        shape(rank + rows, points, dtype=F8),
        shape(rank, points, dtype=F8),
    ]
    lower = None
    near = []
    grams = [None, None]

    def leaf_blocks(blocks, tiles):
        nonlocal kept
        squares = [shape(points, points, dtype=dtype) for dtype in (BF16, F8, F8)]
        out, *kept = call(
            functools.partial(leaf_body, blocks),
            [shape(rows, points), *squares],
            left, right, b, tiles, *kept,
            spaces={3: ANY},
            aliases={4: 1, 5: 2, 6: 3} if kept else None,
        )
        leaf_b.append(out)
        return out

    def make_near(pieces):
        nonlocal near, lower
        holders = [pieces[3][0], pieces[0][0], pieces[2][0], pieces[2][2], pieces[1][0], pieces[1][2]]
        *near, lower = call(
            functools.partial(near_body, feats), [*bigs, shape(rows, rank - TILE)], *holders, right, b
        )
        return lower

    def prepare(tiles):
        nonlocal left, right, b
        left, right, b = call(
            functools.partial(prep_body, feats),
            [shape(points, SIDE, dtype=BF16), shape(SIDE, points, dtype=BF16), shape(rows, points)],
            x, targets, tiles,
            spaces={2: ANY},
        )
        return leaf_blocks(((0, 0), (0, 1), (1, 1)), tiles)

    def make_grams(which, stages, tiles):
        arrays, plan = [], []

        def add(level, near, far):
            plan.append((level, scale[level], len(arrays), len(arrays) + 1))
            arrays.extend((near, far))

        for stage in stages:
            level = STAGES[stage][1]
            own, gots, next_own, other = pieces[stage]
            add(level, own, gots[0])
            if len(gots) == 3:
                add(level, gots[1], gots[2])
                add(level + 1, next_own, other)
        out = shape(len(plan), TILE, TILE, dtype=BF16)
        grams[which] = call(
            functools.partial(gram_body, feats, tuple(plan)), [out, out], me, tiles, *arrays,
            spaces={0: SMEM, 1: ANY},
        )
        return grams[which]

    def last_near(tiles):
        pieces.append((tiles,))
        lower = make_near(pieces)
        pieces.pop()
        return lower, leaf_blocks(((2, 3), (3, 3)), tiles), make_grams(0, (0, 1, 2), tiles)

    work = {
        1: prepare,
        2: functools.partial(leaf_blocks, ((0, 2), (0, 3), (1, 2), (1, 3), (2, 2))),
        3: last_near,
    }
    pieces = []
    tiles = anchors
    for stage, (count, level, masks) in enumerate(STAGES[:LAST]):
        tiles = tiles[:count]
        gots = send(stage, tiles, work.get(stage), masks)
        new = tiles + gots[0]
        other = gots[2] + gots[1] if len(gots) == 3 else None
        pieces.append((tiles, gots, new, other))
        tiles = new if other is None else new + other

    at = 5 + len(leaf_b)
    high, low, high8, low8, message, v, leaf_sum, z_tile, most = call(
        functools.partial(far_body, feats),
        [
            *bigs,
            shape(TILES + 1, rows, TILE),
            *[shape(rows, points)] * 2,
            shape(1, FEATS, TILE),
            shape(rows, TILE),
        ],
        pieces[3][2], tiles, right, b, lower, *leaf_b, *near,
        aliases={at + i: i for i in range(4)},
    )

    def reduce(message, work, extra):
        tiles = message
        mixed = []
        for stage, (count, level, masks) in enumerate(STAGES):
            beside = work.get(stage)
            if beside is not None and stage == LAST:
                beside = functools.partial(beside, mixed)
            gots = send(stage, tiles, beside, masks)
            if stage == LAST:
                return [me, tiles, *gots, *mixed]
            more = extra if stage == LAST - 1 else []
            which, first = ((0, 0), (0, 1), (0, 4), (1, 0))[stage]
            tiles, coefs = call(
                functools.partial(stage_body, stage, first),
                [
                    shape(STAGES[stage + 1][0] + len(more), rows, TILE),
                    shape(rows, RANK if len(masks) == 1 else TILE),
                ],
                me, tiles, *gots[::-1], *grams[which], *more,
                spaces={0: SMEM},
            )
            mixed.append(coefs)

    leaf_near = []

    def near_blocks(blocks, *args):
        nonlocal leaf_near
        tiles = args[-1]
        wide = shape(rank, points, dtype=BF16)
        leaf_near = call(
            functools.partial(leaf_near_body, blocks),
            [wide, wide, shape(rows, points)],
            *kept, high, high8, low8, most, tiles, *leaf_near,
            spaces={7: ANY},
            aliases={8: 0, 9: 1, 10: 2} if leaf_near else None,
        )
        return leaf_near

    def first_near(tiles):
        return make_grams(1, (3,), tiles), near_blocks((0, 1), tiles)

    work = {1: first_near}
    for stage, blocks in ((2, (2, 3)), (3, (4, 5)), (4, (6, 7))):
        work[stage] = functools.partial(near_blocks, blocks)
    ends = reduce(message, work, [z_tile])
    late = shape(TILE, TILE, dtype=BF16)
    message, r, w, ar, keep, *late = call(
        functools.partial(middle_body, feats, scale[7]),
        [shape(TILES + 1, rows, TILE), *[shape(rows, points)] * 3, shape(rows, TILE), late, late],
        *ends, z_tile, b, v, leaf_sum, high, low, *leaf_near,
        spaces={0: SMEM},
    )

    image = None

    def lower_image(mixed, tiles):
        nonlocal image
        (image,) = call(
            image_body, [shape(rows, points)], *mixed, ar, high, low, tiles, spaces={7: ANY}
        )
        return image

    ends = reduce(message, {LAST: lower_image}, [])
    return call(
        last_body, [shape(rows, points)] * 2, *ends, *late, high, low, b, r, w, image, keep, spaces={0: SMEM}
    )


def solution(mesh):
    placed = P(None, "leaf")
    return jax.shard_map(
        shards,
        mesh=mesh,
        in_specs=(placed, placed, placed),
        out_specs=(placed, placed),
        check_vma=False,
    )
```

```python
import functools
import math

import jax
import jax.numpy as jnp
from jax import lax
from jax.experimental import pallas as pl
from jax.experimental.pallas import tpu as pltpu
from jax.sharding import PartitionSpec as P

F32 = jnp.float32
BF16 = jnp.bfloat16
F8 = jnp.float8_e4m3fn
LIFT = 2.0**8
LIFT_LOW = 2.0**16
RANK = 64
TILE = 128
TILES = 4
CHUNKS = 4
SIDE = 256
FEATS = 32
ORDER = (6, 7, 5, 0, 3, 4, 1, 2)
SENT = (7, 0, 5, 6, 3, 4, 1, 2)
PLACE = {level: divmod(spot, 2) for spot, level in enumerate(SENT)}
STAGES = ((4, 0, (1,)), (4, 1, (3, 5, 7)), (3, 3, (9, 17, 25)), (2, 5, (33, 65, 97)), (1, 7, (193,)))
LAST = len(STAGES) - 1
ENDS = 7

VMEM = pl.BlockSpec(memory_space=pltpu.VMEM)
SMEM = pl.BlockSpec(memory_space=pltpu.SMEM)
ANY = pl.BlockSpec(memory_space=pl.ANY)


def call(body, outs, *args, spaces=None, aliases=None, mib=10):
    count = len(args)
    spaces = dict(spaces or {})
    return pl.pallas_call(
        body,
        in_specs=[spaces.get(i, VMEM) for i in range(count)],
        out_specs=(VMEM,) * len(outs),
        out_shape=tuple(outs),
        input_output_aliases=aliases or {},
        compiler_params=pltpu.CompilerParams(vmem_limit_bytes=mib << 20),
    )(*args)


def shape(*dims, dtype=F32):
    return jax.ShapeDtypeStruct(dims, dtype)


def split(x):
    high = x.astype(BF16)
    return high, (x - high.astype(F32)).astype(BF16)


def split3(x):
    high = x.astype(BF16)
    rest = x - high.astype(F32)
    middle = rest.astype(BF16)
    return high, middle, (rest - middle.astype(F32)).astype(BF16)


def eighths(high, low):
    return (high * LIFT).astype(F8), (low * LIFT_LOW).astype(F8)


def dot(a, b):
    return jnp.dot(a, b, preferred_element_type=F32)


def dot_t(a, b):
    return lax.dot_general(a, b, (((1,), (1,)), ((), ())), preferred_element_type=F32)


def stack2(x):
    high, low = split(x)
    return high, jnp.concatenate([high, low], 0)


def three(high, two, u_high, u_low, product=dot):
    rows = high.shape[0]
    first = product(two, u_high)
    return first[:rows] + first[rows:] + product(high, u_low)


def padded(x):
    return jnp.concatenate([x, jnp.zeros((FEATS - x.shape[0], x.shape[1]), F32)], 0)


def both_sides(x, feats):
    x = x * math.sqrt(4.0 * math.log2(math.e) / feats)
    norm = -0.5 * jnp.sum(x * x, 0, keepdims=True)
    one, two, low = split3(x)
    row = lax.broadcasted_iota(jnp.int32, (SIDE - 6 * FEATS, x.shape[1]), 0)
    n1, n2, n3 = (jnp.broadcast_to(n.astype(F32), row.shape) for n in split3(norm))
    norms = jnp.where(row == 0, n1, jnp.where(row == 1, n2, jnp.where(row == 2, n3, 0.0)))
    end_left = jnp.where(row < 3, norms, jnp.where(row < 6, 1.0, 0.0)).astype(BF16)
    norms = jnp.where(row == 3, n1, jnp.where(row == 4, n2, jnp.where(row == 5, n3, 0.0)))
    end_right = jnp.where(row < 3, 1.0, norms).astype(BF16)
    left = jnp.concatenate([one, two, one, two, low, one, end_left], 0)
    right = jnp.concatenate([one, one, two, two, one, low, end_right], 0)
    return left, right


def turned(left):
    return left.astype(F32).T.astype(BF16)


def part(ref, level):
    tile, side = PLACE[level]
    return ref[tile, :, side * RANK : (side + 1) * RANK]


def upper(me_ref, level):
    return (me_ref[0] >> level) & 1 == 1


def pair(me_ref, level, near, far):
    high = upper(me_ref, level)
    return jnp.concatenate([jnp.where(high, far, near), jnp.where(high, near, far)], 1)


def start_body(me_ref, x_ref, index_ref, out_ref, copy_ref):
    x = padded(x_ref[...])
    copy_ref[...] = x
    parts = jnp.concatenate(split3(x), 0)
    points = x_ref.shape[1]
    column = lax.broadcasted_iota(jnp.int32, (1, RANK), 1)
    row = lax.broadcasted_iota(jnp.int32, (points, TILE), 0)
    for tile in range(TILES):
        wanted = []
        for level in SENT[2 * tile : 2 * tile + 2]:
            keep = (1 << level) - 1
            mine = (column & keep) == (me_ref[0] & keep)
            wanted.append(jnp.where(mine, index_ref[level : level + 1, :], -1))
        chosen = jnp.where(row == jnp.concatenate(wanted, 1), 1.0, 0.0).astype(BF16)
        got = dot(parts, chosen)
        out_ref[tile] = got[:FEATS] + got[FEATS : 2 * FEATS] + got[2 * FEATS :]


def prep_body(feats, x_ref, b_ref, _, left_ref, right_ref, copy_ref):
    copy_ref[...] = b_ref[...]
    left, right = both_sides(x_ref[...], feats)
    left_ref[...] = turned(left)
    right_ref[...] = right


def leaf_body(blocks, left_ref, right_ref, b_ref, _, *refs):
    out_ref, high_ref, high8_ref, low8_ref = refs[-4:]
    rows, points = b_ref.shape
    width = points // CHUNKS
    high, two = stack2(b_ref[...])
    totals = [jnp.zeros((rows, width), F32)] * CHUNKS
    spans = [slice(i * width, (i + 1) * width) for i in range(CHUNKS)]
    for i, j in blocks:
        k_high, k_low = split(jnp.exp2(dot(left_ref[spans[i], :], right_ref[:, spans[j]])))
        high_ref[spans[i], spans[j]] = k_high
        high8_ref[spans[i], spans[j]], low8_ref[spans[i], spans[j]] = eighths(k_high, k_low)
        totals[j] = totals[j] + three(high[:, spans[i]], two[:, spans[i]], k_high, k_low)
        if i != j:
            totals[i] = totals[i] + three(high[:, spans[j]], two[:, spans[j]], k_high, k_low, dot_t)
    for span, total in zip(spans, totals):
        out_ref[:, span] = total


def gram_body(feats, plan, me_ref, _, *refs):
    *refs, high_ref, low_ref = refs
    for index, (level, scale, near, far) in enumerate(plan):
        both = pair(me_ref, level, part(refs[near], level), part(refs[far], level))
        left, right = both_sides(both, feats)
        gram = jnp.exp2(dot(turned(left), right)) * scale
        high_ref[index], low_ref[index] = split(gram)


def near_tile(left, first, right_ref, b_ref, high_ref, low_ref, high8_ref, low8_ref):
    rows, points = b_ref.shape
    width = points // CHUNKS
    count = left.shape[0]
    total = jnp.zeros((rows, count), F32)
    for chunk in range(CHUNKS):
        here = slice(chunk * width, (chunk + 1) * width)
        u_high, u_low = split(jnp.exp2(dot(left, right_ref[:, here])))
        at = slice(first, first + count)
        high_ref[at, here], low_ref[at, here] = u_high, u_low
        high8_ref[at, here], low8_ref[at, here] = eighths(u_high, u_low)
        b_high, two = stack2(b_ref[:, here])
        total = total + three(b_high, two, u_high, u_low, dot_t)
    return total


def near_body(feats, *refs):
    z_refs, (right_ref, b_ref), (*near_refs, out_ref) = refs[:6], refs[6:8], refs[8:]
    z = jnp.concatenate([part(ref, level) for ref, level in zip(z_refs, ORDER[2:])], 1)
    left = turned(both_sides(z, feats)[0])
    out_ref[...] = near_tile(left, TILE, right_ref, b_ref, *near_refs)


def put_tiles(out_ref, total):
    for tile in range(TILES):
        halves = []
        for level in SENT[2 * tile : 2 * tile + 2]:
            at = ORDER.index(level) * RANK
            halves.append(total[:, at : at + RANK])
        out_ref[tile] = jnp.concatenate(halves, 1)


def far_body(feats, z6_ref, z7_ref, right_ref, b_ref, lower_ref, *refs):
    leaf_refs, near_refs, (out_ref, v_ref, leaf_ref, z_ref, most_ref) = refs[:-13], refs[-9:-5], refs[-5:]
    rank = TILES * TILE
    rows = b_ref.shape[0]
    z = jnp.concatenate([part(z6_ref, 6), part(z7_ref, 7)], 1)
    z_ref[0] = z
    left = turned(both_sides(z, feats)[0])
    total = near_tile(left, 0, right_ref, b_ref, *near_refs)
    put_tiles(out_ref, jnp.concatenate([total, lower_ref[...]], 1))
    b = b_ref[...]
    leaf = leaf_refs[0][...]
    for ref in leaf_refs[1:]:
        leaf = leaf + ref[...]
    leaf_ref[...] = leaf
    v = b + 0.25 * leaf
    v_ref[...] = v
    most = jnp.max(jnp.abs(v), 1, keepdims=True)
    most = jnp.where(most > 0.0, most, 1.0)
    most_ref[...] = jnp.broadcast_to(most, most_ref.shape)
    high_ref, _, high8_ref, _ = near_refs
    _, v_two = stack2(v)
    high_ref[rank:, :] = v_two
    high8_ref[rank:, :] = (v * (LIFT / most)).astype(F8)
    bv = jnp.sum(b * v, 1, keepdims=True)
    bb = jnp.sum(b * b, 1, keepdims=True)
    lane = lax.broadcasted_iota(jnp.int32, (rows, TILE), 1)
    out_ref[TILES] = jnp.where(lane == 0, bv, jnp.where(lane == 1, bb, 0.0))


def leaf_near_body(blocks, k_ref, k_high8_ref, k_low8_ref, high_ref, high8_ref, low8_ref, most_ref, _, *refs):
    out_high_ref, out_low_ref, out_v_ref = refs[-3:]
    points = k_ref.shape[0]
    width = points // CHUNKS
    rank = TILES * TILE
    rows = out_v_ref.shape[0]
    for block in blocks:
        span = slice(block * SIDE, (block + 1) * SIDE)
        end = (block * SIDE // width + 1) * width
        out = dot(high_ref[:, :end], k_ref[:end, span])
        second = dot(high8_ref[:, :end], k_low8_ref[:end, span])
        other = dot(low8_ref[:, :end], k_high8_ref[:end, span])
        if end < points:
            out = out + dot_t(high_ref[:, end:], k_ref[span, end:])
            second = second + dot_t(high8_ref[:, end:], k_low8_ref[span, end:])
            other = other + dot_t(low8_ref[:, end:], k_high8_ref[span, end:])
        scale = 1.0 / (LIFT * LIFT_LOW)
        out_high_ref[:, span], out_low_ref[:, span] = split(out[:rank] + (second[:rank] + other) * scale)
        last = out[rank : rank + rows] + out[rank + rows :]
        out_v_ref[:, span] = last + (most_ref[:, :1] * scale) * second[rank:]


def mix(me_ref, level, near, far, gram):
    both = pair(me_ref, level, near, far)
    high, two = stack2(both)
    image = three(high, two, *gram)
    total = jnp.sum(image * both, 1, keepdims=True)
    mine = jnp.where(upper(me_ref, level), image[:, RANK:], image[:, :RANK])
    return mine, total


def sum_stage(stage, me_ref, tiles, gots, grams):
    count, level, masks = STAGES[stage]
    mine, total = mix(me_ref, level, part(tiles, level), part(gots[0], level), grams[0])
    mixed = [mine]
    new = [tiles[i] + gots[0][i] for i in range(count)]
    if len(masks) == 3:
        _, more = mix(me_ref, level, part(gots[1], level), part(gots[2], level), grams[1])
        total = total + more
        other = [gots[1][i] + gots[2][i] for i in range(count)]
        tile, side = PLACE[level + 1]
        here = slice(side * RANK, (side + 1) * RANK)
        mine, more = mix(me_ref, level + 1, new[tile][:, here], other[tile][:, here], grams[2])
        mixed.append(mine)
        total = total + more
        new = [a + b for a, b in zip(new, other)]
    return new, mixed, total


def with_scalar(tile, total):
    lane = lax.broadcasted_iota(jnp.int32, tile.shape, 1)
    return tile + jnp.where(lane == RANK, total, 0.0)


def stage_body(stage, first, me_ref, *refs):
    masks = STAGES[stage][2]
    tiles, gots = refs[0], refs[1 : 1 + len(masks)][::-1]
    high_ref, low_ref, *more, out_ref, mixed_ref = refs[1 + len(masks) :]
    grams = [(high_ref[first + i], low_ref[first + i]) for i in range(len(masks))]
    new, mixed, total = sum_stage(stage, me_ref, tiles, gots, grams)
    if stage == 0:
        scalars = tiles[TILES] + gots[0][TILES]
        new[0] = jnp.concatenate([new[0][:, :RANK], scalars[:, :RANK]], 1)
    new[0] = with_scalar(new[0], total)
    for tile in range(STAGES[stage + 1][0]):
        out_ref[tile] = new[tile]
    for ref in more:
        out_ref[STAGES[stage + 1][0]] = ref[0]
    mixed_ref[...] = mixed[0] if len(mixed) == 1 else jnp.concatenate(mixed, 1)


def last_stage(refs, late):
    me_ref, tiles, got, m0_ref, m12_ref, m34_ref, m56_ref = refs
    new, (m7,), total = sum_stage(LAST, me_ref, tiles, [got], [late])
    scalars = with_scalar(new[0], total)[:, RANK:]
    m5, m6 = m56_ref[:, :RANK], m56_ref[:, RANK:]
    return scalars, jnp.concatenate([m6, m7, m5, m0_ref[...], m34_ref[...], m12_ref[...]], 1)


def middle_body(feats, scale, *refs):
    ends, refs = refs[:ENDS], refs[ENDS:]
    z_ref, b_ref, v_ref, leaf_ref, high_ref, low_ref, near_high_ref, near_low_ref, near_v_ref = refs[:9]
    out_ref, r_ref, w_ref, ar_ref, keep_ref, late_high_ref, late_low_ref = refs[9:]
    here = slice(RANK, 2 * RANK)
    both = pair(ends[0], STAGES[LAST][1], z_ref[0][:, here], ends[2][1][:, here])
    left, right = both_sides(both, feats)
    late = split(jnp.exp2(dot(turned(left), right)) * scale)
    late_high_ref[...], late_low_ref[...] = late
    scalars, mixed = last_stage(ends, late)
    bab, bb = scalars[:, 0:1], scalars[:, 1:2]
    alpha = bb / bab
    m_high, m_two = stack2(mixed)
    rows, points = b_ref.shape
    width = points // CHUNKS
    rank = TILES * TILE
    rar = rr = rw = jnp.zeros((rows, 1), F32)
    totals = jnp.zeros((rows, rank), F32)
    for chunk in range(CHUNKS):
        here = slice(chunk * width, (chunk + 1) * width)
        high, low = high_ref[:rank, here], low_ref[:rank, here]
        w = v_ref[:, here] + three(m_high, m_two, high, low)
        r = b_ref[:, here] - alpha * w
        r_ref[:, here] = r
        w_ref[:, here] = w
        r_high, r_two = stack2(r)
        totals = totals + three(r_high, r_two, high, low, dot_t)
        leaf_w = near_v_ref[:, here] + three(m_high, m_two, near_high_ref[:, here], near_low_ref[:, here])
        ar = r + 0.25 * (leaf_ref[:, here] - alpha * leaf_w)
        ar_ref[:, here] = ar
        rar = rar + jnp.sum(r * ar, 1, keepdims=True)
        rr = rr + jnp.sum(r * r, 1, keepdims=True)
        rw = rw + jnp.sum(r * w, 1, keepdims=True)
    lane = lax.broadcasted_iota(jnp.int32, (rows, TILE), 1)
    put_tiles(out_ref, totals)
    out_ref[TILES] = jnp.where(
        lane == 0, rar, jnp.where(lane == 1, rr, jnp.where(lane == 2, rw, 0.0))
    )
    keep_ref[...] = jnp.where(lane == 0, alpha, jnp.where(lane == 1, bab, jnp.where(lane == 2, bb, 0.0)))


def image_body(m0_ref, m12_ref, m34_ref, m56_ref, ar_ref, high_ref, low_ref, _, out_ref):
    m5, m6 = m56_ref[:, :RANK], m56_ref[:, RANK:]
    mixed = [m6, jnp.zeros_like(m6), m5, m0_ref[...], m34_ref[...], m12_ref[...]]
    m_high, m_two = stack2(jnp.concatenate(mixed, 1))
    rank = TILES * TILE
    width = ar_ref.shape[1] // CHUNKS
    for chunk in range(CHUNKS):
        here = slice(chunk * width, (chunk + 1) * width)
        out_ref[:, here] = ar_ref[:, here] + three(m_high, m_two, high_ref[:rank, here], low_ref[:rank, here])


def last_body(*refs):
    ends, late, refs = refs[:ENDS], refs[ENDS : ENDS + 2], refs[ENDS + 2 :]
    high_ref, low_ref, b_ref, r_ref, w_ref, image_ref, keep_ref, x_ref, out_ref = refs
    scalars, mixed = last_stage(ends, [ref[...] for ref in late])
    rar, rr, rw = scalars[:, 0:1], scalars[:, 1:2], scalars[:, 2:3]
    alpha, bab, bb = keep_ref[:, 0:1], keep_ref[:, 1:2], keep_ref[:, 2:3]
    beta = rr / bb
    alpha_next = rr / (rar + beta * (2.0 * rw + beta * bab))
    m7 = mixed[:, RANK : 2 * RANK]
    m_high, m_two = stack2(jnp.concatenate([jnp.zeros_like(m7), m7], 1))
    width = b_ref.shape[1] // CHUNKS
    for chunk in range(CHUNKS):
        here = slice(chunk * width, (chunk + 1) * width)
        r, b = r_ref[:, here], b_ref[:, here]
        image = image_ref[:, here] + three(m_high, m_two, high_ref[:TILE, here], low_ref[:TILE, here])
        image = image + beta * w_ref[:, here]
        x_ref[:, here] = alpha * b + alpha_next * (r + beta * b)
        out_ref[:, here] = r - alpha_next * image


def swapped(block, mask):
    count = lax.axis_size("leaf")
    return lax.ppermute(block, "leaf", [(i, i ^ mask) for i in range(count)])


def send(stage, tiles, work, masks):
    got = [swapped(tiles, mask) for mask in masks[::-1]]
    if work is not None:
        *got, _ = lax.optimization_barrier((*got, work(tiles)))
    return got[::-1]


def shards(coordinates, targets, anchor_index):
    feats, points = coordinates.shape
    rows = targets.shape[0]
    width = points // CHUNKS
    rank = TILES * TILE
    b = None
    me = lax.axis_index("leaf").astype(jnp.int32).reshape(1)
    scale = {level: 512.0 / (RANK * (1 << level) * points) for level in ORDER}

    anchors, x = call(
        start_body,
        [shape(TILES, FEATS, TILE), shape(FEATS, points)],
        me, coordinates, anchor_index,
        spaces={0: SMEM},
    )

    left = right = None
    leaf_b = []
    kept = []
    bigs = [
        shape(rank + 2 * rows, points, dtype=BF16),
        shape(rank, points, dtype=BF16),
        shape(rank + rows, points, dtype=F8),
        shape(rank, points, dtype=F8),
    ]
    lower = None
    near = []
    grams = [None, None]

    def leaf_blocks(blocks, tiles):
        nonlocal kept
        squares = [shape(points, points, dtype=dtype) for dtype in (BF16, F8, F8)]
        out, *kept = call(
            functools.partial(leaf_body, blocks),
            [shape(rows, points), *squares],
            left, right, b, tiles, *kept,
            spaces={3: ANY},
            aliases={4: 1, 5: 2, 6: 3} if kept else None,
        )
        leaf_b.append(out)
        return out

    def make_near(pieces):
        nonlocal near, lower
        holders = [pieces[3][0], pieces[0][0], pieces[2][0], pieces[2][2], pieces[1][0], pieces[1][2]]
        *near, lower = call(
            functools.partial(near_body, feats), [*bigs, shape(rows, rank - TILE)], *holders, right, b
        )
        return lower

    def prepare(tiles):
        nonlocal left, right, b
        left, right, b = call(
            functools.partial(prep_body, feats),
            [shape(points, SIDE, dtype=BF16), shape(SIDE, points, dtype=BF16), shape(rows, points)],
            x, targets, tiles,
            spaces={2: ANY},
        )
        return leaf_blocks(((0, 0), (0, 1), (1, 1)), tiles)

    def make_grams(which, stages, tiles):
        arrays, plan = [], []

        def add(level, near, far):
            plan.append((level, scale[level], len(arrays), len(arrays) + 1))
            arrays.extend((near, far))

        for stage in stages:
            level = STAGES[stage][1]
            own, gots, next_own, other = pieces[stage]
            add(level, own, gots[0])
            if len(gots) == 3:
                add(level, gots[1], gots[2])
                add(level + 1, next_own, other)
        out = shape(len(plan), TILE, TILE, dtype=BF16)
        grams[which] = call(
            functools.partial(gram_body, feats, tuple(plan)), [out, out], me, tiles, *arrays,
            spaces={0: SMEM, 1: ANY},
        )
        return grams[which]

    def last_near(tiles):
        pieces.append((tiles,))
        lower = make_near(pieces)
        pieces.pop()
        return lower, leaf_blocks(((2, 3), (3, 3)), tiles), make_grams(0, (0, 1, 2), tiles)

    work = {
        1: prepare,
        2: functools.partial(leaf_blocks, ((0, 2), (0, 3), (1, 2), (1, 3), (2, 2))),
        3: last_near,
    }
    pieces = []
    tiles = anchors
    for stage, (count, level, masks) in enumerate(STAGES[:LAST]):
        tiles = tiles[:count]
        gots = send(stage, tiles, work.get(stage), masks)
        new = tiles + gots[0]
        other = gots[2] + gots[1] if len(gots) == 3 else None
        pieces.append((tiles, gots, new, other))
        tiles = new if other is None else new + other

    at = 5 + len(leaf_b)
    high, low, high8, low8, message, v, leaf_sum, z_tile, most = call(
        functools.partial(far_body, feats),
        [
            *bigs,
            shape(TILES + 1, rows, TILE),
            *[shape(rows, points)] * 2,
            shape(1, FEATS, TILE),
            shape(rows, TILE),
        ],
        pieces[3][2], tiles, right, b, lower, *leaf_b, *near,
        aliases={at + i: i for i in range(4)},
    )

    def reduce(message, work, extra):
        tiles = message
        mixed = []
        for stage, (count, level, masks) in enumerate(STAGES):
            beside = work.get(stage)
            if beside is not None and stage == LAST:
                beside = functools.partial(beside, mixed)
            gots = send(stage, tiles, beside, masks)
            if stage == LAST:
                return [me, tiles, *gots, *mixed]
            more = extra if stage == LAST - 1 else []
            which, first = ((0, 0), (0, 1), (0, 4), (1, 0))[stage]
            tiles, coefs = call(
                functools.partial(stage_body, stage, first),
                [
                    shape(STAGES[stage + 1][0] + len(more), rows, TILE),
                    shape(rows, RANK if len(masks) == 1 else TILE),
                ],
                me, tiles, *gots[::-1], *grams[which], *more,
                spaces={0: SMEM},
            )
            mixed.append(coefs)

    leaf_near = []

    def near_blocks(blocks, *args):
        nonlocal leaf_near
        tiles = args[-1]
        wide = shape(rank, points, dtype=BF16)
        leaf_near = call(
            functools.partial(leaf_near_body, blocks),
            [wide, wide, shape(rows, points)],
            *kept, high, high8, low8, most, tiles, *leaf_near,
            spaces={7: ANY},
            aliases={8: 0, 9: 1, 10: 2} if leaf_near else None,
        )
        return leaf_near

    def first_near(tiles):
        return make_grams(1, (3,), tiles), near_blocks((0, 1), tiles)

    work = {1: first_near}
    for stage, blocks in ((2, (2, 3)), (3, (4, 5)), (4, (6, 7))):
        work[stage] = functools.partial(near_blocks, blocks)
    ends = reduce(message, work, [z_tile])
    late = shape(TILE, TILE, dtype=BF16)
    message, r, w, ar, keep, *late = call(
        functools.partial(middle_body, feats, scale[7]),
        [shape(TILES + 1, rows, TILE), *[shape(rows, points)] * 3, shape(rows, TILE), late, late],
        *ends, z_tile, b, v, leaf_sum, high, low, *leaf_near,
        spaces={0: SMEM},
    )

    image = None

    def lower_image(mixed, tiles):
        nonlocal image
        (image,) = call(
            image_body, [shape(rows, points)], *mixed, ar, high, low, tiles, spaces={7: ANY}
        )
        return image

    ends = reduce(message, {LAST: lower_image}, [])
    return call(
        last_body, [shape(rows, points)] * 2, *ends, *late, high, low, b, r, w, image, keep, spaces={0: SMEM}
    )


def solution(mesh):
    placed = P(None, "leaf")
    return jax.shard_map(
        shards,
        mesh=mesh,
        in_specs=(placed, placed, placed),
        out_specs=(placed, placed),
        check_vma=False,
    )
```
